256 devices in a mesh: row: 16 (over z_hi, y, core), col: 16 (over z_lo, x).
Axes of the slice: x: 4, y: 4, z: 8 (z_hi: 2, z_lo: 4; z = z_hi * 4 + z_lo), core: 2. Of those that a mesh axis runs over, the one named last changes fastest.
Arguments:
- activations: bfloat16 [4, 2048, 5120], P(None, None, 'row'), may hold values from -6 to 6
- out_grads: bfloat16 [4, 2048, 13824], P(None, 'row', 'col'), may hold values from -6 to 6
- hash_seeds: int32 [2], replicated, may hold values from 0 to 1073741823
- offsets: int32 [2], replicated, may hold values from 0 to 1048575
Outputs:
- features: float32 [4, 32, 64], P(None, 'col', 'row')
The draws below stay inside these ranges and needn't reach their ends.
All inputs are finite; a program needn't handle non-finite values.
Results may differ from the reference program's by a relative error of at most 0.0041.
Values sent between devices are 32-bit elements; how exact they have to be, the bound alone decides.
No kernel may reach another device: no remote copies, remote signals or barrier semaphores. Data moves between devices by JAX's collectives and lax.ppermute only.
A program may use at most 64 MiB of HBM per device.

```python
import math
import jax
import jax.numpy as jnp
from jax import lax

D = 5120
FF = 13824
K_IN = 32
K_OUT = 64
SEQ_LEN = 2048
SEQS = 4


def levels(stream_key, shape, pieces, low, largest):
    gain = 1.0
    for position, parts in pieces:
        steps = jax.random.uniform(jax.random.fold_in(jax.random.fold_in(stream_key, 6), position), (parts,), jnp.float32, low / len(pieces), largest / len(pieces))
        gain = gain * jnp.repeat(jnp.exp(steps), shape[position] // parts).reshape((-1,) + (1,) * (len(shape) - 1 - position))
    return gain


def bell_draw(key, dims, deviation, bound, split=(), kind=jnp.bfloat16):
    result = deviation * jax.random.normal(key, dims, jnp.float32)
    if split:
        result = result * levels(key, dims, split, -0.22, 0.18)
    return jnp.clip(result, -bound, bound).astype(kind)


def setup_inputs(seed: int = 0) -> dict:
    streams_of = jax.random.split(jax.random.key(seed), 5)
    return {
        "activations": bell_draw(streams_of[0], (SEQS, SEQ_LEN, D), 1.0, 6.0, ((2, 16),)),
        "out_grads": bell_draw(streams_of[1], (SEQS, SEQ_LEN, FF), 1.0, 6.0, ((1, 16), (2, 16))),
        "hash_seeds": jax.random.randint(streams_of[2], (2,), 0, 1073741824).astype(jnp.int32),
        "offsets": jax.random.randint(streams_of[3], (2,), 0, 1048576).astype(jnp.int32),
    }


def scramble(counter, seed_value):
    hashed = jnp.bitwise_xor(counter, seed_value)
    shift_by = jnp.full_like(hashed, 16)
    hashed = hashed * jnp.int32(73244475)
    hashed = jnp.bitwise_xor(hashed, lax.shift_right_logical(hashed, shift_by))
    hashed = hashed * jnp.int32(73244475)
    hashed = jnp.bitwise_xor(hashed, lax.shift_right_logical(hashed, shift_by))
    return hashed

def unit_draw(hashed):
    top_bits = lax.shift_right_logical(hashed, jnp.full_like(hashed, 8))
    return (top_bits.astype(jnp.float32) + 0.5) * (1.0 / 16777216.0)

def normal_table(seed_value, offset, first_row, row_count, first_col, col_count, stride, fan_in):
    row_ids = first_row + lax.broadcasted_iota(jnp.int32, (row_count, col_count), 0)
    col_ids = first_col + lax.broadcasted_iota(jnp.int32, (row_count, col_count), 1)
    counter = offset + row_ids * stride + col_ids
    radius = jnp.sqrt(-2.0 * jnp.log(unit_draw(scramble(2 * counter, seed_value))))
    angle_part = unit_draw(scramble(2 * counter + 1, seed_value))
    normal_values = radius * jnp.cos(2.0 * math.pi * angle_part) * fan_in ** (-0.5)
    return normal_values.astype(jnp.bfloat16)

def reference(activations, out_grads, hash_seeds, offsets):
    in_table = normal_table(hash_seeds[0], offsets[0], 0, D, 0, K_IN, K_IN, D)
    out_table = normal_table(hash_seeds[1], offsets[1], 0, FF, 0, K_OUT, K_OUT, FF)
    input_side = jnp.dot(activations.reshape(SEQS * SEQ_LEN, D), in_table, preferred_element_type=jnp.float32)
    input_side = input_side.reshape(SEQS, SEQ_LEN, K_IN)
    output_side = jnp.dot(out_grads.reshape(SEQS * SEQ_LEN, FF), out_table, preferred_element_type=jnp.float32)
    output_side = output_side.reshape(SEQS, SEQ_LEN, K_OUT)
    features = jnp.einsum('sti,stj->sij', input_side, output_side, precision=lax.Precision.HIGHEST)
    return features * SEQ_LEN ** (-0.5)
```

```python
import functools

import jax
import jax.numpy as jnp
from jax import lax
from jax.experimental import pallas as pl
from jax.experimental.pallas import tpu as pltpu
from jax.sharding import PartitionSpec as P

D = 5120
FF = 13824
K_IN = 32
K_OUT = 64
SEQ_LEN = 2048
SEQS = 4
ROWS = 16
COLS = 16
LANES = 128
MULTIPLIER = 73244475
VMEM_LIMIT = 60 * 1024 * 1024

SIN_TURN = (
    6.283185280154403,
    -41.34168061334532,
    81.60247636883796,
    -76.5811726421402,
    39.75982706857711,
)


def scramble(counter, seed_value):
    hashed = counter ^ seed_value
    hashed = hashed * jnp.int32(MULTIPLIER)
    hashed = hashed ^ lax.shift_right_logical(hashed, jnp.full_like(hashed, 16))
    hashed = hashed * jnp.int32(MULTIPLIER)
    return hashed ^ lax.shift_right_logical(hashed, jnp.full_like(hashed, 16))


def unit_draw(hashed):
    top_bits = lax.shift_right_logical(hashed, jnp.full_like(hashed, 8))
    return (top_bits.astype(jnp.float32) + 0.5) * (1.0 / 16777216.0)


def cos_turn(angle):
    quarter = jnp.abs(angle - 0.5) - 0.25
    square = quarter * quarter
    total = jnp.full_like(square, SIN_TURN[-1])
    for term in SIN_TURN[-2::-1]:
        total = total * square + term
    return total * quarter


def normal_draw(counter, seed_value, fan_in):
    radius = jnp.sqrt(-2.0 * jnp.log(unit_draw(scramble(2 * counter, seed_value))))
    angle = unit_draw(scramble(2 * counter + 1, seed_value))
    return (radius * cos_turn(angle) * fan_in ** (-0.5)).astype(jnp.bfloat16)


def input_kernel(seeds, offsets, acts, terms, held, arrived):
    row = lax.axis_index("row")
    seq = lax.rem(lax.axis_index("col"), SEQS)
    here = acts.shape[1]
    fetch = pltpu.make_async_copy(acts.at[seq], held, arrived)
    fetch.start()
    shape = (K_IN, here)
    slot = lax.broadcasted_iota(jnp.int32, shape, 0)
    feature = row * here + lax.broadcasted_iota(jnp.int32, shape, 1)
    factor = (slot & 15) * 2 + lax.shift_right_logical(slot, jnp.full_like(slot, 4))
    table = normal_draw(offsets[0] + feature * K_IN + factor, seeds[0], D)
    fetch.wait()
    for part in range(4):
        product = jnp.dot(
            table, held[:, part * 512 : (part + 1) * 512], preferred_element_type=jnp.float32
        )
        for piece in range(4):
            terms[part * 4 + piece] = product[:, piece * LANES : (piece + 1) * LANES]


def output_kernel(seeds, offsets, grads, own, near, far, both, held, arrived):
    col = lax.axis_index("col")
    seq = lax.rem(col, SEQS)
    here = grads.shape[1]
    fetches = []
    for m in range(SEQS):
        fetch = pltpu.make_async_copy(grads.at[seq ^ m], held.at[m], arrived.at[m])
        fetch.start()
        fetches.append(fetch)
    shape = (K_OUT, here)
    factor = lax.broadcasted_iota(jnp.int32, shape, 0)
    feature = col * here + lax.broadcasted_iota(jnp.int32, shape, 1)
    table = normal_draw(offsets[1] + feature * K_OUT + factor, seeds[1], FF)
    for m, out in ((3, both), (2, far), (1, near), (0, own)):
        fetches[m].wait()
        out[...] = jnp.dot(table, held[m], preferred_element_type=jnp.float32)


def feature_kernel(terms, own, near, far, both, spread):
    side_in = terms[0]
    for r in range(1, ROWS):
        side_in = side_in + terms[r]
    side_out = (own[...] + near[...]) + (far[...] + both[...])
    halves = [
        lax.dot_general(
            side_in[b * 16 : (b + 1) * 16],
            side_out,
            (((1,), (1,)), ((), ())),
            precision=lax.Precision.HIGHEST,
            preferred_element_type=jnp.float32,
        )
        for b in range(2)
    ]
    paired = jnp.concatenate(halves, axis=1) * SEQ_LEN ** (-0.5)
    for r in range(ROWS):
        shifted = paired if r == 0 else pltpu.roll(paired, LANES - 4 * r, 1)
        spread[r * COLS : (r + 1) * COLS] = shifted


def body(activations, out_grads, hash_seeds, offsets):
    acts = jnp.swapaxes(activations, 1, 2)
    grads = jnp.swapaxes(out_grads, 1, 2)
    here_in = acts.shape[1]
    here_out = grads.shape[1]
    smem = pl.BlockSpec(memory_space=pltpu.SMEM)
    vmem = pl.BlockSpec(memory_space=pltpu.VMEM)
    anywhere = pl.BlockSpec(memory_space=pl.ANY)
    params = pltpu.CompilerParams(vmem_limit_bytes=VMEM_LIMIT)

    side = jax.ShapeDtypeStruct((K_OUT, LANES), jnp.float32)
    own, near, far, both = pl.pallas_call(
        output_kernel,
        out_shape=[side] * 4,
        in_specs=[smem, smem, anywhere],
        out_specs=[vmem] * 4,
        scratch_shapes=[
            pltpu.VMEM((SEQS, here_out, LANES), jnp.bfloat16),
            pltpu.SemaphoreType.DMA((SEQS,)),
        ],
        compiler_params=params,
        name="output_terms",
    )(hash_seeds, offsets, grads)
    terms = pl.pallas_call(
        input_kernel,
        out_shape=jax.ShapeDtypeStruct((ROWS, K_IN, LANES), jnp.float32),
        in_specs=[smem, smem, anywhere],
        out_specs=vmem,
        scratch_shapes=[
            pltpu.VMEM((here_in, SEQ_LEN), jnp.bfloat16),
            pltpu.SemaphoreType.DMA,
        ],
        compiler_params=params,
        name="input_terms",
    )(hash_seeds, offsets, acts)

    def across(value, distance):
        return lax.ppermute(value, "col", [(c, c ^ distance) for c in range(COLS)])

    near, far, both = across(near, 1), across(far, 2), across(both, 3)
    terms = lax.all_to_all(terms, "row", 0, 0, tiled=True)
    spread = pl.pallas_call(
        feature_kernel,
        out_shape=jax.ShapeDtypeStruct((ROWS * COLS, LANES), jnp.float32),
        in_specs=[vmem] * 5,
        out_specs=vmem,
        compiler_params=params,
        name="feature_partials",
    )(terms, own, near, far, both)
    spread = lax.all_to_all(spread, ("row", "col"), 0, 0, tiled=True)
    summed = jnp.sum(spread.reshape(ROWS * COLS // SEQS, SEQS, LANES), axis=0)
    return summed.reshape(SEQS, 2, K_OUT)[:, :, :4]


def solution(mesh):
    return jax.shard_map(
        body,
        mesh=mesh,
        in_specs=(P(None, None, "row"), P(None, "row", "col"), P(), P()),
        out_specs=P(None, "col", "row"),
        check_vma=False,
    )
```

```python
import jax
import jax.numpy as jnp
from jax import lax
from jax.experimental import pallas as pl
from jax.experimental.pallas import tpu as pltpu
from jax.sharding import Mesh, PartitionSpec as P

D = 5120
FF = 13824
K_IN = 32
K_OUT = 64
SEQ_LEN = 2048
SEQS = 4
LANES = 128
BLOCKS = SEQ_LEN // LANES
IN_HERE = 8
OUT_HERE = 32
MULTIPLIER = 73244475
AXES = ("zh", "y", "core", "zl", "x")
SIZES = (2, 4, 2, 4, 4)
ROW = ("zh", "y", "core")
COL = ("zl", "x")

SIN_TURN = (
    6.283185280154403,
    -41.34168061334532,
    81.60247636883796,
    -76.5811726421402,
    39.75982706857711,
)


def scramble(counter, seed_value):
    hashed = counter ^ seed_value
    hashed = hashed * jnp.int32(MULTIPLIER)
    hashed = hashed ^ lax.shift_right_logical(hashed, jnp.full_like(hashed, 16))
    hashed = hashed * jnp.int32(MULTIPLIER)
    return hashed ^ lax.shift_right_logical(hashed, jnp.full_like(hashed, 16))


def unit_draw(hashed):
    top_bits = lax.shift_right_logical(hashed, jnp.full_like(hashed, 8))
    return (top_bits.astype(jnp.float32) + 0.5) * (1.0 / 16777216.0)


def cos_turn(angle):
    quarter = jnp.abs(angle - 0.5) - 0.25
    square = quarter * quarter
    total = jnp.full_like(square, SIN_TURN[-1])
    for term in SIN_TURN[-2::-1]:
        total = total * square + term
    return total * quarter


def normal_draw(counter, seed_value, fan_in):
    radius = jnp.sqrt(-2.0 * jnp.log(unit_draw(scramble(2 * counter, seed_value))))
    angle = unit_draw(scramble(2 * counter + 1, seed_value))
    return (radius * cos_turn(angle) * fan_in ** (-0.5)).astype(jnp.bfloat16)


def input_kernel(seeds, offsets, acts, send, keep, held, blocks, arrived):
    zh, y, core, zl, x = (lax.axis_index(axis) for axis in AXES)
    here = acts.shape[1]
    fetch = pltpu.make_async_copy(acts.at[x], held, arrived)
    fetch.start()
    shape = (IN_HERE, here)
    factor = zl * IN_HERE + lax.broadcasted_iota(jnp.int32, shape, 0)
    row = (zh * 4 + y) * 2 + core
    feature = row * here + lax.broadcasted_iota(jnp.int32, shape, 1)
    table = normal_draw(offsets[0] + feature * K_IN + factor, seeds[0], D)
    fetch.wait()
    for part in range(4):
        product = jnp.dot(
            table, held[:, part * 512 : (part + 1) * 512], preferred_element_type=jnp.float32
        )
        for piece in range(4):
            blocks[part * 4 + piece] = product[:, piece * LANES : (piece + 1) * LANES]
    for out, other in ((send, core ^ 1), (keep, core)):
        for b in range(2):
            for c in range(2):
                for z in range(2):
                    out[b, c, z] = blocks[(z * 4 + (y ^ b ^ (3 * c))) * 2 + other]


def output_kernel(seeds, offsets, grads, send, keep):
    zl, x = (lax.axis_index(axis) for axis in COL)
    here = grads.shape[1]
    shape = (K_OUT, here)
    factor = lax.broadcasted_iota(jnp.int32, shape, 0)
    feature = (zl * 4 + x) * here + lax.broadcasted_iota(jnp.int32, shape, 1)
    table = normal_draw(offsets[1] + feature * K_OUT + factor, seeds[1], FF)
    for b, out in ((1, send), (0, keep)):
        for c in range(2):
            out[c] = jnp.dot(
                table, grads[x ^ b ^ (3 * c)], preferred_element_type=jnp.float32
            )


def pack_kernel(in_own, in_other, out_own, out_other, packed):
    side_in = in_own[0] + in_other[...]
    side_out = out_own[0] + out_other[...]
    for dest in range(8):
        half = (dest // 4) * OUT_HERE
        packed[dest, :OUT_HERE] = side_out[half : half + OUT_HERE]
        for z in range(2):
            start = OUT_HERE + z * IN_HERE
            packed[dest, start : start + IN_HERE] = side_in[z]


def feature_kernel(packed, spread):
    zl = lax.axis_index("zl")
    total = None
    for z in range(2):
        source = z * 4
        side_out = (packed[source, :OUT_HERE] + packed[source + 1, :OUT_HERE]) + (
            packed[source + 2, :OUT_HERE] + packed[source + 3, :OUT_HERE]
        )
        start = OUT_HERE + z * IN_HERE
        rows = pl.ds(start, IN_HERE)
        side_in = packed[zl, rows, :] + packed[4 + zl, rows, :]
        product = lax.dot_general(
            side_in,
            jnp.concatenate([side_out] * 4, axis=0),
            (((1,), (1,)), ((), ())),
            precision=lax.Precision.HIGHEST,
            preferred_element_type=jnp.float32,
        )
        total = product if total is None else total + product
    total = total * SEQ_LEN ** (-0.5)
    for place in range(8):
        spread[place] = total if place == 0 else pltpu.roll(total, LANES - 4 * place, 1)


def body(activations, out_grads, hash_seeds, offsets):
    acts = jnp.swapaxes(activations, 1, 2)
    grads = jnp.swapaxes(out_grads, 1, 2)
    here_in = acts.shape[1]
    smem = pl.BlockSpec(memory_space=pltpu.SMEM)
    vmem = pl.BlockSpec(memory_space=pltpu.VMEM)
    small = pltpu.CompilerParams(vmem_limit_bytes=16 * 1024 * 1024)

    def shaped(*dims):
        return jax.ShapeDtypeStruct(dims, jnp.float32)

    def swap(value, axis, distance):
        size = SIZES[AXES.index(axis)]
        return lax.ppermute(value, axis, [(i, i ^ distance) for i in range(size)])

    in_send, in_keep = pl.pallas_call(
        input_kernel,
        out_shape=[shaped(2, 2, 2, IN_HERE, LANES)] * 2,
        in_specs=[smem, smem, pl.BlockSpec(memory_space=pl.ANY)],
        out_specs=[vmem] * 2,
        scratch_shapes=[
            pltpu.VMEM((here_in, SEQ_LEN), jnp.bfloat16),
            pltpu.VMEM((BLOCKS, IN_HERE, LANES), jnp.float32),
            pltpu.SemaphoreType.DMA,
        ],
        compiler_params=pltpu.CompilerParams(vmem_limit_bytes=60 * 1024 * 1024),
        name="input_terms",
    )(hash_seeds, offsets, acts)
    in_got = swap(in_send, "core", 1)
    out_send, out_keep = pl.pallas_call(
        output_kernel,
        out_shape=[shaped(2, K_OUT, LANES)] * 2,
        in_specs=[smem, smem, vmem],
        out_specs=[vmem] * 2,
        compiler_params=small,
        name="output_terms",
    )(hash_seeds, offsets, grads)
    in_sum = in_keep + in_got
    in_pair = in_sum[0] + swap(in_sum[1], "y", 1)
    out_pair = out_keep + swap(out_send, "x", 1)
    in_got = swap(in_pair[1], "y", 3)
    out_got = swap(out_pair[1], "x", 3)
    packed = pl.pallas_call(
        pack_kernel,
        out_shape=shaped(8, OUT_HERE + 2 * IN_HERE, LANES),
        in_specs=[vmem] * 4,
        out_specs=vmem,
        compiler_params=small,
        name="pack_sides",
    )(in_pair, in_got, out_pair, out_got)
    packed = lax.all_to_all(packed, ("zh", "zl"), 0, 0, tiled=True)
    spread = pl.pallas_call(
        feature_kernel,
        out_shape=shaped(8, 8, LANES),
        in_specs=[vmem],
        out_specs=vmem,
        compiler_params=small,
        name="feature_partials",
    )(packed)
    spread = lax.all_to_all(
        spread.reshape(32, 2, LANES), ("y", "core", "x"), 0, 0, tiled=True
    )
    summed = jnp.sum(spread.reshape(8, SEQS, 2, LANES), axis=0)
    return summed[:, :, :4]


def solution(mesh):
    fine = Mesh(mesh.devices.reshape(SIZES), AXES)
    return jax.shard_map(
        body,
        mesh=fine,
        in_specs=(P(None, None, ROW), P(None, ROW, COL), P(), P()),
        out_specs=P(None, COL, ROW),
        check_vma=False,
    )
```

```python
import jax
import jax.numpy as jnp
from jax import lax
from jax.experimental import pallas as pl
from jax.experimental.pallas import tpu as pltpu
from jax.sharding import Mesh, PartitionSpec as P

D = 5120
FF = 13824
K_IN = 32
K_OUT = 64
SEQ_LEN = 2048
SEQS = 4
LANES = 128
BLOCKS = SEQ_LEN // LANES
IN_HERE = 8
IN_SENT = 16
PARTS = 2
PART = SEQ_LEN // 2 // PARTS
OUT_HERE = 32
MULTIPLIER = 73244475
AXES = ("zh", "y", "core", "zl", "x")
SIZES = (2, 4, 2, 4, 4)
ROW = ("zh", "y", "core")
COL = ("zl", "x")

SIN_TURN = (
    6.283185280154403,
    -41.34168061334532,
    81.60247636883796,
    -76.5811726421402,
    39.75982706857711,
)


def scramble(counter, seed_value):
    hashed = counter ^ seed_value
    hashed = hashed * jnp.int32(MULTIPLIER)
    hashed = hashed ^ lax.shift_right_logical(hashed, jnp.full_like(hashed, 16))
    hashed = hashed * jnp.int32(MULTIPLIER)
    return hashed ^ lax.shift_right_logical(hashed, jnp.full_like(hashed, 16))


def unit_draw(hashed):
    top_bits = lax.shift_right_logical(hashed, jnp.full_like(hashed, 8))
    return (top_bits.astype(jnp.float32) + 0.5) * (1.0 / 16777216.0)


def cos_turn(angle):
    quarter = jnp.abs(angle - 0.5) - 0.25
    square = quarter * quarter
    total = jnp.full_like(square, SIN_TURN[-1])
    for term in SIN_TURN[-2::-1]:
        total = total * square + term
    return total * quarter


def normal_draw(counter, seed_value, fan_in):
    radius = jnp.sqrt(-2.0 * jnp.log(unit_draw(scramble(2 * counter, seed_value))))
    angle = unit_draw(scramble(2 * counter + 1, seed_value))
    return (radius * cos_turn(angle) * fan_in ** (-0.5)).astype(jnp.bfloat16)


def input_kernel(
    seeds_hbm, offsets_hbm, acts, send, keep, seeds, offsets, held, blocks, arrived, told
):
    zh, y, core, zl, x = (lax.axis_index(axis) for axis in AXES)
    here = acts.shape[1]
    half = lax.shift_right_logical(zl, 1)
    tell = [
        pltpu.make_async_copy(seeds_hbm, seeds, told.at[0]),
        pltpu.make_async_copy(offsets_hbm, offsets, told.at[1]),
    ]
    for copy in tell:
        copy.start()
    fetches = []
    for part in range(PARTS):
        start = pl.multiple_of(half * (SEQ_LEN // 2) + part * PART, PART)
        fetch = pltpu.make_async_copy(
            acts.at[x, :, pl.ds(start, PART)], held.at[part], arrived.at[part]
        )
        fetch.start()
        fetches.append(fetch)
    for copy in tell:
        copy.wait()
    shape = (IN_SENT, here)
    factor = (zl & 1) * IN_SENT + lax.broadcasted_iota(jnp.int32, shape, 0)
    row = (zh * 4 + y) * 2 + core
    feature = row * here + lax.broadcasted_iota(jnp.int32, shape, 1)
    table = normal_draw(offsets[0] + feature * K_IN + factor, seeds[0], D)
    for part in range(PARTS):
        fetches[part].wait()
        product = jnp.dot(table, held[part], preferred_element_type=jnp.float32)
        for piece in range(PART // LANES):
            blocks[part * (PART // LANES) + piece] = product[
                :, piece * LANES : (piece + 1) * LANES
            ]
    for out, other in ((send, core ^ 1), (keep, core)):
        for b in range(2):
            for c in range(2):
                out[b, c] = blocks[(y ^ b ^ (3 * c)) * 2 + other]


def output_kernel(seeds, offsets, grads, after, send, keep):
    zl, x = (lax.axis_index(axis) for axis in COL)
    here = grads.shape[1]
    shape = (K_OUT, here)
    factor = lax.broadcasted_iota(jnp.int32, shape, 0)
    feature = (zl * 4 + x) * here + lax.broadcasted_iota(jnp.int32, shape, 1)
    table = normal_draw(offsets[1] + feature * K_OUT + factor, seeds[1], FF)
    for b, out in ((1, send), (0, keep)):
        for c in range(2):
            out[c] = jnp.dot(
                table, grads[x ^ b ^ (3 * c)], preferred_element_type=jnp.float32
            )


def add_kernel(own, got, after, send, keep):
    keep[...] = own[0] + got[0]
    send[...] = own[1] + got[1]


def pack_kernel(in_own, in_got, out_own, out_got, packed):
    side_in = in_own[...] + in_got[...]
    side_out = out_own[...] + out_got[...]
    for dest in range(8):
        half = (dest // 4) * OUT_HERE
        packed[dest, :OUT_HERE] = side_out[half : half + OUT_HERE]
        half = (dest % 2) * IN_HERE
        packed[dest, OUT_HERE:] = side_in[half : half + IN_HERE]


def feature_kernel(packed, spread):
    factor_half = lax.shift_right_logical(lax.axis_index("zl"), 1)
    total = None
    for z in range(2):
        source = z * 4
        side_out = (packed[source, :OUT_HERE] + packed[source + 1, :OUT_HERE]) + (
            packed[source + 2, :OUT_HERE] + packed[source + 3, :OUT_HERE]
        )
        source = z * 2 + factor_half
        side_in = packed[source, OUT_HERE:] + packed[4 + source, OUT_HERE:]
        product = lax.dot_general(
            side_in,
            jnp.concatenate([side_out] * 4, axis=0),
            (((1,), (1,)), ((), ())),
            precision=lax.Precision.HIGHEST,
            preferred_element_type=jnp.float32,
        )
        total = product if total is None else total + product
    total = total * SEQ_LEN ** (-0.5)
    for place in range(8):
        spread[place] = total if place == 0 else pltpu.roll(total, LANES - 4 * place, 1)


def body(activations, out_grads, hash_seeds, offsets):
    acts = jnp.swapaxes(activations, 1, 2)
    grads = jnp.swapaxes(out_grads, 1, 2)
    here_in = acts.shape[1]
    smem = pl.BlockSpec(memory_space=pltpu.SMEM)
    vmem = pl.BlockSpec(memory_space=pltpu.VMEM)
    hbm = pl.BlockSpec(memory_space=pltpu.HBM)
    anywhere = pl.BlockSpec(memory_space=pl.ANY)
    params = pltpu.CompilerParams(vmem_limit_bytes=16 * 1024 * 1024)

    def shaped(*dims):
        return jax.ShapeDtypeStruct(dims, jnp.float32)

    def pinned(value):
        return pltpu.with_memory_space_constraint(value, pltpu.HBM)

    def swap(value, axis, distance):
        size = SIZES[AXES.index(axis)]
        return lax.ppermute(value, axis, [(i, i ^ distance) for i in range(size)])

    def add(own, got, after, name):
        return pl.pallas_call(
            add_kernel,
            out_shape=[shaped(*own.shape[1:])] * 2,
            in_specs=[vmem, vmem, anywhere],
            out_specs=[vmem] * 2,
            compiler_params=params,
            name=name,
        )(own, got, after)

    in_send, in_keep = pl.pallas_call(
        input_kernel,
        out_shape=[shaped(2, 2, IN_SENT, LANES)] * 2,
        in_specs=[hbm] * 3,
        out_specs=[vmem] * 2,
        scratch_shapes=[
            pltpu.SMEM((2,), jnp.int32),
            pltpu.SMEM((2,), jnp.int32),
            pltpu.VMEM((PARTS, here_in, PART), jnp.bfloat16),
            pltpu.VMEM((BLOCKS // 2, IN_SENT, LANES), jnp.float32),
            pltpu.SemaphoreType.DMA((PARTS,)),
            pltpu.SemaphoreType.DMA((2,)),
        ],
        compiler_params=params,
        name="input_terms",
    )(pinned(hash_seeds), pinned(offsets), pinned(acts))
    in_got = swap(in_send, "core", 1)
    out_send, out_keep = pl.pallas_call(
        output_kernel,
        out_shape=[shaped(2, K_OUT, LANES)] * 2,
        in_specs=[smem, smem, vmem, anywhere],
        out_specs=[vmem] * 2,
        compiler_params=params,
        name="output_terms",
    )(hash_seeds, offsets, grads, in_send)
    in_send, in_keep = add(in_keep, in_got, out_send, "add_core")
    in_got = swap(in_send, "y", 1)
    out_got = swap(out_send, "x", 1)
    in_send, in_keep = add(in_keep, in_got, in_got, "add_y")
    in_got = swap(in_send, "y", 3)
    out_send, out_keep = add(out_keep, out_got, in_send, "add_x")
    out_got = swap(out_send, "x", 3)
    packed = pl.pallas_call(
        pack_kernel,
        out_shape=shaped(8, OUT_HERE + IN_HERE, LANES),
        in_specs=[vmem] * 4,
        out_specs=vmem,
        compiler_params=params,
        name="pack_sides",
    )(in_keep, in_got, out_keep, out_got)
    packed = lax.all_to_all(packed, ("zh", "zl"), 0, 0, tiled=True)
    spread = pl.pallas_call(
        feature_kernel,
        out_shape=shaped(8, 8, LANES),
        in_specs=[vmem],
        out_specs=vmem,
        compiler_params=params,
        name="feature_partials",
    )(packed)
    spread = lax.all_to_all(
        spread.reshape(32, 2, LANES), ("y", "core", "x"), 0, 0, tiled=True
    )
    summed = jnp.sum(spread.reshape(8, SEQS, 2, LANES), axis=0)
    return summed[:, :, :4]


def solution(mesh):
    fine = Mesh(mesh.devices.reshape(SIZES), AXES)
    return jax.shard_map(
        body,
        mesh=fine,
        in_specs=(P(None, None, ROW), P(None, ROW, COL), P(), P()),
        out_specs=P(None, COL, ROW),
        check_vma=False,
    )
```

```python
import jax
import jax.numpy as jnp
from jax import lax
from jax.experimental import pallas as pl
from jax.experimental.pallas import tpu as pltpu
from jax.sharding import Mesh, PartitionSpec as P

D = 5120
FF = 13824
K_IN = 32
K_OUT = 64
SEQ_LEN = 2048
SEQS = 4
LANES = 128
BLOCKS = SEQ_LEN // LANES
IN_HERE = 8
IN_SENT = 16
PARTS = 2
PART = SEQ_LEN // 2 // PARTS
OUT_HERE = 32
MULTIPLIER = 73244475
AXES = ("zh", "y", "core", "zl", "x")
SIZES = (2, 4, 2, 4, 4)
ROW = ("zh", "y", "core")
COL = ("zl", "x")

SIN_TURN = (
    6.283185280154403,
    -41.34168061334532,
    81.60247636883796,
    -76.5811726421402,
    39.75982706857711,
)


def scramble(counter, seed_value):
    hashed = counter ^ seed_value
    hashed = hashed * jnp.int32(MULTIPLIER)
    hashed = hashed ^ lax.shift_right_logical(hashed, jnp.full_like(hashed, 16))
    hashed = hashed * jnp.int32(MULTIPLIER)
    return hashed ^ lax.shift_right_logical(hashed, jnp.full_like(hashed, 16))


def unit_draw(hashed):
    top_bits = lax.shift_right_logical(hashed, jnp.full_like(hashed, 8))
    return (top_bits.astype(jnp.float32) + 0.5) * (1.0 / 16777216.0)


def cos_turn(angle):
    quarter = jnp.abs(angle - 0.5) - 0.25
    square = quarter * quarter
    total = jnp.full_like(square, SIN_TURN[-1])
    for term in SIN_TURN[-2::-1]:
        total = total * square + term
    return total * quarter


def normal_draw(counter, seed_value, fan_in):
    radius = jnp.sqrt(-2.0 * jnp.log(unit_draw(scramble(2 * counter, seed_value))))
    angle = unit_draw(scramble(2 * counter + 1, seed_value))
    return (radius * cos_turn(angle) * fan_in ** (-0.5)).astype(jnp.bfloat16)


def input_kernel(
    seeds_hbm, offsets_hbm, acts, send, keep, seeds, offsets, held, blocks, arrived, told
):
    zh, y, core, zl, x = (lax.axis_index(axis) for axis in AXES)
    here = acts.shape[1]
    half = lax.shift_right_logical(zl, 1)
    tell = [
        pltpu.make_async_copy(seeds_hbm, seeds, told.at[0]),
        pltpu.make_async_copy(offsets_hbm, offsets, told.at[1]),
    ]
    for copy in tell:
        copy.start()
    fetches = []
    for part in range(PARTS):
        start = pl.multiple_of(half * (SEQ_LEN // 2) + part * PART, PART)
        fetch = pltpu.make_async_copy(
            acts.at[x, :, pl.ds(start, PART)], held.at[part], arrived.at[part]
        )
        fetch.start()
        fetches.append(fetch)
    for copy in tell:
        copy.wait()
    shape = (IN_SENT, here)
    factor = (zl & 1) * IN_SENT + lax.broadcasted_iota(jnp.int32, shape, 0)
    row = (zh * 4 + y) * 2 + core
    feature = row * here + lax.broadcasted_iota(jnp.int32, shape, 1)
    table = normal_draw(offsets[0] + feature * K_IN + factor, seeds[0], D)
    for part in range(PARTS):
        fetches[part].wait()
        product = jnp.dot(table, held[part], preferred_element_type=jnp.float32)
        for piece in range(PART // LANES):
            blocks[part * (PART // LANES) + piece] = product[
                :, piece * LANES : (piece + 1) * LANES
            ]
    for out, other in ((send, core ^ 1), (keep, core)):
        for b in range(2):
            for c in range(2):
                out[b, c] = blocks[(y ^ b ^ (3 * c)) * 2 + other]


def output_kernel(seeds, offsets, grads, after, send, keep):
    zl, x = (lax.axis_index(axis) for axis in COL)
    here = grads.shape[1]
    shape = (K_OUT, here)
    factor = lax.broadcasted_iota(jnp.int32, shape, 0)
    feature = (zl * 4 + x) * here + lax.broadcasted_iota(jnp.int32, shape, 1)
    table = normal_draw(offsets[1] + feature * K_OUT + factor, seeds[1], FF)
    for b, out in ((1, send), (0, keep)):
        for c in range(2):
            out[c] = jnp.dot(
                table, grads[x ^ b ^ (3 * c)], preferred_element_type=jnp.float32
            )


def add_kernel(own, got, after, send, keep):
    keep[...] = own[0] + got[0]
    send[...] = own[1] + got[1]


def add_through_kernel(own, got, passed, send, keep, handed_on):
    keep[...] = own[0] + got[0]
    send[...] = own[1] + got[1]


def pack_kernel(in_own, in_got, out_own, out_got, packed):
    side_in = in_own[...] + in_got[...]
    side_out = out_own[...] + out_got[...]
    for dest in range(8):
        half = (dest // 4) * OUT_HERE
        packed[dest, :OUT_HERE] = side_out[half : half + OUT_HERE]
        half = (dest % 2) * IN_HERE
        packed[dest, OUT_HERE:] = side_in[half : half + IN_HERE]


def feature_kernel(packed, spread):
    factor_half = lax.shift_right_logical(lax.axis_index("zl"), 1)
    total = None
    for z in range(2):
        source = z * 4
        side_out = (packed[source, :OUT_HERE] + packed[source + 1, :OUT_HERE]) + (
            packed[source + 2, :OUT_HERE] + packed[source + 3, :OUT_HERE]
        )
        source = z * 2 + factor_half
        side_in = packed[source, OUT_HERE:] + packed[4 + source, OUT_HERE:]
        product = lax.dot_general(
            side_in,
            jnp.concatenate([side_out] * 4, axis=0),
            (((1,), (1,)), ((), ())),
            precision=lax.Precision.HIGHEST,
            preferred_element_type=jnp.float32,
        )
        total = product if total is None else total + product
    total = total * SEQ_LEN ** (-0.5)
    for place in range(8):
        spread[place] = total if place == 0 else pltpu.roll(total, LANES - 4 * place, 1)


def body(activations, out_grads, hash_seeds, offsets):
    acts = jnp.swapaxes(activations, 1, 2)
    grads = jnp.swapaxes(out_grads, 1, 2)
    here_in = acts.shape[1]
    smem = pl.BlockSpec(memory_space=pltpu.SMEM)
    vmem = pl.BlockSpec(memory_space=pltpu.VMEM)
    hbm = pl.BlockSpec(memory_space=pltpu.HBM)
    anywhere = pl.BlockSpec(memory_space=pl.ANY)
    params = pltpu.CompilerParams(vmem_limit_bytes=16 * 1024 * 1024)

    def shaped(*dims):
        return jax.ShapeDtypeStruct(dims, jnp.float32)

    def pinned(value):
        return pltpu.with_memory_space_constraint(value, pltpu.HBM)

    def swap(value, axis, distance):
        size = SIZES[AXES.index(axis)]
        return lax.ppermute(value, axis, [(i, i ^ distance) for i in range(size)])

    def add(own, got, after, name):
        return pl.pallas_call(
            add_kernel,
            out_shape=[shaped(*own.shape[1:])] * 2,
            in_specs=[vmem, vmem, anywhere],
            out_specs=[vmem] * 2,
            compiler_params=params,
            name=name,
        )(own, got, after)

    in_send, in_keep = pl.pallas_call(
        input_kernel,
        out_shape=[shaped(2, 2, IN_SENT, LANES)] * 2,
        in_specs=[hbm] * 3,
        out_specs=[vmem] * 2,
        scratch_shapes=[
            pltpu.SMEM((2,), jnp.int32),
            pltpu.SMEM((2,), jnp.int32),
            pltpu.VMEM((PARTS, here_in, PART), jnp.bfloat16),
            pltpu.VMEM((BLOCKS // 2, IN_SENT, LANES), jnp.float32),
            pltpu.SemaphoreType.DMA((PARTS,)),
            pltpu.SemaphoreType.DMA((2,)),
        ],
        compiler_params=params,
        name="input_terms",
    )(pinned(hash_seeds), pinned(offsets), pinned(acts))
    in_got = swap(in_send, "core", 1)
    out_send, out_keep = pl.pallas_call(
        output_kernel,
        out_shape=[shaped(2, K_OUT, LANES)] * 2,
        in_specs=[smem, smem, vmem, anywhere],
        out_specs=[vmem] * 2,
        compiler_params=params,
        name="output_terms",
    )(hash_seeds, offsets, grads, in_send)
    in_send, in_keep, out_send = pl.pallas_call(
        add_through_kernel,
        out_shape=[shaped(2, IN_SENT, LANES)] * 2 + [shaped(2, K_OUT, LANES)],
        in_specs=[vmem, vmem, anywhere],
        out_specs=[vmem, vmem, anywhere],
        input_output_aliases={2: 2},
        compiler_params=params,
        name="add_core",
    )(in_keep, in_got, out_send)
    in_got = swap(in_send, "y", 1)
    out_got = swap(out_send, "x", 1)
    in_send, in_keep = add(in_keep, in_got, in_got, "add_y")
    in_got = swap(in_send, "y", 3)
    out_send, out_keep = add(out_keep, out_got, in_send, "add_x")
    out_got = swap(out_send, "x", 3)
    packed = pl.pallas_call(
        pack_kernel,
        out_shape=shaped(8, OUT_HERE + IN_HERE, LANES),
        in_specs=[vmem] * 4,
        out_specs=vmem,
        compiler_params=params,
        name="pack_sides",
    )(in_keep, in_got, out_keep, out_got)
    packed = lax.all_to_all(packed, ("zh", "zl"), 0, 0, tiled=True)
    spread = pl.pallas_call(
        feature_kernel,
        out_shape=shaped(8, 8, LANES),
        in_specs=[vmem],
        out_specs=vmem,
        compiler_params=params,
        name="feature_partials",
    )(packed)
    spread = lax.all_to_all(
        spread.reshape(32, 2, LANES), ("y", "core", "x"), 0, 0, tiled=True
    )
    summed = jnp.sum(spread.reshape(8, SEQS, 2, LANES), axis=0)
    return summed[:, :, :4]


def solution(mesh):
    fine = Mesh(mesh.devices.reshape(SIZES), AXES)
    return jax.shard_map(
        body,
        mesh=fine,
        in_specs=(P(None, None, ROW), P(None, ROW, COL), P(), P()),
        out_specs=P(None, COL, ROW),
        check_vma=False,
    )
```

```python
import jax
import jax.numpy as jnp
from jax import lax
from jax.experimental import pallas as pl
from jax.experimental.pallas import tpu as pltpu
from jax.sharding import Mesh, PartitionSpec as P

D = 5120
FF = 13824
K_IN = 32
K_OUT = 64
SEQ_LEN = 2048
SEQS = 4
LANES = 128
BLOCKS = SEQ_LEN // LANES
IN_HERE = 8
IN_SENT = 16
PARTS = 2
PART = SEQ_LEN // 2 // PARTS
OUT_HERE = 32
MULTIPLIER = 73244475
AXES = ("zh", "y", "core", "zl", "x")
SIZES = (2, 4, 2, 4, 4)
ROW = ("zh", "y", "core")
COL = ("zl", "x")

SIN_TURN = (
    6.283185280154403,
    -41.34168061334532,
    81.60247636883796,
    -76.5811726421402,
    39.75982706857711,
)


def scramble(counter, seed_value):
    hashed = counter ^ seed_value
    hashed = hashed * jnp.int32(MULTIPLIER)
    hashed = hashed ^ lax.shift_right_logical(hashed, jnp.full_like(hashed, 16))
    hashed = hashed * jnp.int32(MULTIPLIER)
    return hashed ^ lax.shift_right_logical(hashed, jnp.full_like(hashed, 16))


def unit_draw(hashed):
    top_bits = lax.shift_right_logical(hashed, jnp.full_like(hashed, 8))
    return (top_bits.astype(jnp.float32) + 0.5) * (1.0 / 16777216.0)


def cos_turn(angle):
    quarter = jnp.abs(angle - 0.5) - 0.25
    square = quarter * quarter
    total = jnp.full_like(square, SIN_TURN[-1])
    for term in SIN_TURN[-2::-1]:
        total = total * square + term
    return total * quarter


def normal_draw(counter, seed_value, fan_in):
    radius = jnp.sqrt(-2.0 * jnp.log(unit_draw(scramble(2 * counter, seed_value))))
    angle = unit_draw(scramble(2 * counter + 1, seed_value))
    return (radius * cos_turn(angle) * fan_in ** (-0.5)).astype(jnp.bfloat16)


def input_kernel(
    seeds_hbm, offsets_hbm, acts, send, keep, seeds, offsets, held, blocks, arrived, told
):
    zh, y, core, zl, x = (lax.axis_index(axis) for axis in AXES)
    here = acts.shape[1]
    half = lax.shift_right_logical(zl, 1)
    tell = [
        pltpu.make_async_copy(seeds_hbm, seeds, told.at[0]),
        pltpu.make_async_copy(offsets_hbm, offsets, told.at[1]),
    ]
    for copy in tell:
        copy.start()
    fetches = []
    for part in range(PARTS):
        start = pl.multiple_of(half * (SEQ_LEN // 2) + part * PART, PART)
        fetch = pltpu.make_async_copy(
            acts.at[x, :, pl.ds(start, PART)], held.at[part], arrived.at[part]
        )
        fetch.start()
        fetches.append(fetch)
    for copy in tell:
        copy.wait()
    shape = (IN_SENT, here)
    factor = (zl & 1) * IN_SENT + lax.broadcasted_iota(jnp.int32, shape, 0)
    row = (zh * 4 + y) * 2 + core
    feature = row * here + lax.broadcasted_iota(jnp.int32, shape, 1)
    table = normal_draw(offsets[0] + feature * K_IN + factor, seeds[0], D)
    for part in range(PARTS):
        fetches[part].wait()
        product = jnp.dot(table, held[part], preferred_element_type=jnp.float32)
        for piece in range(PART // LANES):
            blocks[part * (PART // LANES) + piece] = product[
                :, piece * LANES : (piece + 1) * LANES
            ]
    for out, other in ((send, core ^ 1), (keep, core)):
        for b in range(2):
            for c in range(2):
                out[b, c] = blocks[(y ^ b ^ (3 * c)) * 2 + other]


def output_kernel(seeds, offsets, grads, after, send, keep):
    zl, x = (lax.axis_index(axis) for axis in COL)
    here = grads.shape[1]
    shape = (K_OUT, here)
    factor = lax.broadcasted_iota(jnp.int32, shape, 0)
    feature = (zl * 4 + x) * here + lax.broadcasted_iota(jnp.int32, shape, 1)
    table = normal_draw(offsets[1] + feature * K_OUT + factor, seeds[1], FF)
    for b, out in ((1, send), (0, keep)):
        for c in range(2):
            out[c] = jnp.dot(
                table, grads[x ^ b ^ (3 * c)], preferred_element_type=jnp.float32
            )


def add_kernel(own, got, after, send, keep):
    keep[...] = own[0] + got[0]
    send[...] = own[1] + got[1]


def add_through_kernel(own, got, passed, send, keep, handed_on):
    keep[...] = own[0] + got[0]
    send[...] = own[1] + got[1]


def pack_kernel(in_own, in_got, out_own, out_got, packed):
    side_in = in_own[...] + in_got[...]
    side_out = out_own[...] + out_got[...]
    for dest in range(8):
        half = (dest // 4) * OUT_HERE
        packed[dest, :OUT_HERE] = side_out[half : half + OUT_HERE]
        half = (dest % 2) * IN_HERE
        packed[dest, OUT_HERE:] = side_in[half : half + IN_HERE]


def feature_kernel(packed, spread):
    factor_half = lax.shift_right_logical(lax.axis_index("zl"), 1)
    sides_in, sides_out = [], []
    for z in range(2):
        source = z * 4
        sides_out.append(
            (packed[source, :OUT_HERE] + packed[source + 1, :OUT_HERE])
            + (packed[source + 2, :OUT_HERE] + packed[source + 3, :OUT_HERE])
        )
        source = z * 2 + factor_half
        sides_in.append(packed[source, OUT_HERE:] + packed[4 + source, OUT_HERE:])
    product = lax.dot_general(
        jnp.concatenate(sides_in, axis=1) * SEQ_LEN ** (-0.5),
        jnp.concatenate(sides_out, axis=1),
        (((1,), (1,)), ((), ())),
        precision=lax.Precision.HIGHEST,
        preferred_element_type=jnp.float32,
    )
    total = jnp.concatenate(
        [product, jnp.zeros((IN_HERE, LANES - OUT_HERE), jnp.float32)], axis=1
    )
    for place in range(8):
        spread[place] = total if place == 0 else pltpu.roll(total, LANES - 4 * place, 1)


def sum_kernel(parts, features):
    total = parts[0]
    for place in range(1, 8):
        total = total + parts[place]
    for seq in range(SEQS):
        features[seq] = total[2 * seq : 2 * seq + 2, :4]


def body(activations, out_grads, hash_seeds, offsets):
    acts = jnp.swapaxes(activations, 1, 2)
    grads = jnp.swapaxes(out_grads, 1, 2)
    here_in = acts.shape[1]
    smem = pl.BlockSpec(memory_space=pltpu.SMEM)
    vmem = pl.BlockSpec(memory_space=pltpu.VMEM)
    hbm = pl.BlockSpec(memory_space=pltpu.HBM)
    anywhere = pl.BlockSpec(memory_space=pl.ANY)
    params = pltpu.CompilerParams(vmem_limit_bytes=16 * 1024 * 1024)

    def shaped(*dims):
        return jax.ShapeDtypeStruct(dims, jnp.float32)

    def pinned(value):
        return pltpu.with_memory_space_constraint(value, pltpu.HBM)

    def swap(value, axis, distance):
        size = SIZES[AXES.index(axis)]
        return lax.ppermute(value, axis, [(i, i ^ distance) for i in range(size)])

    def add(own, got, after, name):
        return pl.pallas_call(
            add_kernel,
            out_shape=[shaped(*own.shape[1:])] * 2,
            in_specs=[vmem, vmem, anywhere],
            out_specs=[vmem] * 2,
            compiler_params=params,
            name=name,
        )(own, got, after)

    in_send, in_keep = pl.pallas_call(
        input_kernel,
        out_shape=[shaped(2, 2, IN_SENT, LANES)] * 2,
        in_specs=[hbm] * 3,
        out_specs=[vmem] * 2,
        scratch_shapes=[
            pltpu.SMEM((2,), jnp.int32),
            pltpu.SMEM((2,), jnp.int32),
            pltpu.VMEM((PARTS, here_in, PART), jnp.bfloat16),
            pltpu.VMEM((BLOCKS // 2, IN_SENT, LANES), jnp.float32),
            pltpu.SemaphoreType.DMA((PARTS,)),
            pltpu.SemaphoreType.DMA((2,)),
        ],
        compiler_params=params,
        name="input_terms",
    )(pinned(hash_seeds), pinned(offsets), pinned(acts))
    in_got = swap(in_send, "core", 1)
    out_send, out_keep = pl.pallas_call(
        output_kernel,
        out_shape=[shaped(2, K_OUT, LANES)] * 2,
        in_specs=[smem, smem, vmem, anywhere],
        out_specs=[vmem] * 2,
        compiler_params=params,
        name="output_terms",
    )(hash_seeds, offsets, grads, in_send)
    in_send, in_keep, out_send = pl.pallas_call(
        add_through_kernel,
        out_shape=[shaped(2, IN_SENT, LANES)] * 2 + [shaped(2, K_OUT, LANES)],
        in_specs=[vmem, vmem, anywhere],
        out_specs=[vmem, vmem, anywhere],
        input_output_aliases={2: 2},
        compiler_params=params,
        name="add_core",
    )(in_keep, in_got, out_send)
    in_got = swap(in_send, "y", 1)
    out_got = swap(out_send, "x", 1)
    in_send, in_keep = add(in_keep, in_got, in_got, "add_y")
    in_got = swap(in_send, "y", 3)
    out_send, out_keep = add(out_keep, out_got, in_send, "add_x")
    out_got = swap(out_send, "x", 3)
    packed = pl.pallas_call(
        pack_kernel,
        out_shape=shaped(8, OUT_HERE + IN_HERE, LANES),
        in_specs=[vmem] * 4,
        out_specs=vmem,
        compiler_params=params,
        name="pack_sides",
    )(in_keep, in_got, out_keep, out_got)
    packed = lax.all_to_all(packed, ("zh", "zl"), 0, 0, tiled=True)
    spread = pl.pallas_call(
        feature_kernel,
        out_shape=shaped(8, 8, LANES),
        in_specs=[vmem],
        out_specs=vmem,
        compiler_params=params,
        name="feature_partials",
    )(packed)
    spread = lax.all_to_all(
        spread.reshape(32, 2, LANES), ("y", "core", "x"), 0, 0, tiled=True
    )
    summed = jnp.sum(spread.reshape(8, SEQS, 2, LANES), axis=0)
    return summed[:, :, :4]


def solution(mesh):
    fine = Mesh(mesh.devices.reshape(SIZES), AXES)
    return jax.shard_map(
        body,
        mesh=fine,
        in_specs=(P(None, None, ROW), P(None, ROW, COL), P(), P()),
        out_specs=P(None, COL, ROW),
        check_vma=False,
    )
```

```python
import jax
import jax.numpy as jnp
from jax import lax
from jax.experimental import pallas as pl
from jax.experimental.pallas import tpu as pltpu
from jax.sharding import Mesh, PartitionSpec as P

D = 5120
FF = 13824
K_IN = 32
K_OUT = 64
SEQ_LEN = 2048
SEQS = 4
LANES = 128
BLOCKS = SEQ_LEN // LANES
IN_HERE = 8
IN_SENT = 16
SENT_ROWS = 40
PARTS = 2
PART = SEQ_LEN // 2 // PARTS
OUT_HERE = 32
MULTIPLIER = 73244475
AXES = ("zh", "y", "core", "zl", "x")
SIZES = (2, 4, 2, 4, 4)
ROW = ("zh", "y", "core")
COL = ("zl", "x")

SIN_TURN = (
    6.283185280154403,
    -41.34168061334532,
    81.60247636883796,
    -76.5811726421402,
    39.75982706857711,
)


def scramble(counter, seed_value):
    hashed = counter ^ seed_value
    hashed = hashed * jnp.int32(MULTIPLIER)
    hashed = hashed ^ lax.shift_right_logical(hashed, jnp.full_like(hashed, 16))
    hashed = hashed * jnp.int32(MULTIPLIER)
    return hashed ^ lax.shift_right_logical(hashed, jnp.full_like(hashed, 16))


def unit_draw(hashed):
    top_bits = lax.shift_right_logical(hashed, jnp.full_like(hashed, 8))
    return (top_bits.astype(jnp.float32) + 0.5) * (1.0 / 16777216.0)


def cos_turn(angle):
    quarter = jnp.abs(angle - 0.5) - 0.25
    square = quarter * quarter
    total = jnp.full_like(square, SIN_TURN[-1])
    for term in SIN_TURN[-2::-1]:
        total = total * square + term
    return total * quarter


def normal_draw(counter, seed_value, fan_in):
    radius = jnp.sqrt(-2.0 * jnp.log(unit_draw(scramble(2 * counter, seed_value))))
    angle = unit_draw(scramble(2 * counter + 1, seed_value))
    return (radius * cos_turn(angle) * fan_in ** (-0.5)).astype(jnp.bfloat16)


def input_kernel(
    seeds_hbm, offsets_hbm, acts, send, keep, out_table, seeds, offsets, held, blocks, arrived, told
):
    zh, y, core, zl, x = (lax.axis_index(axis) for axis in AXES)
    here = acts.shape[1]
    half = lax.shift_right_logical(zl, 1)
    tell = [
        pltpu.make_async_copy(seeds_hbm, seeds, told.at[0]),
        pltpu.make_async_copy(offsets_hbm, offsets, told.at[1]),
    ]
    for copy in tell:
        copy.start()
    fetches = []
    for part in range(PARTS):
        start = pl.multiple_of(half * (SEQ_LEN // 2) + part * PART, PART)
        fetch = pltpu.make_async_copy(
            acts.at[x, :, pl.ds(start, PART)], held.at[part], arrived.at[part]
        )
        fetch.start()
        fetches.append(fetch)
    for copy in tell:
        copy.wait()
    shape = (IN_SENT, here)
    factor = (zl & 1) * IN_SENT + lax.broadcasted_iota(jnp.int32, shape, 0)
    row = (zh * 4 + y) * 2 + core
    feature = row * here + lax.broadcasted_iota(jnp.int32, shape, 1)
    table = normal_draw(offsets[0] + feature * K_IN + factor, seeds[0], D)
    shape = out_table.shape
    factor = lax.broadcasted_iota(jnp.int32, shape, 0)
    feature = (zl * 4 + x) * shape[1] + lax.broadcasted_iota(jnp.int32, shape, 1)
    out_table[...] = normal_draw(offsets[1] + feature * K_OUT + factor, seeds[1], FF)
    for part in range(PARTS):
        fetches[part].wait()
        product = jnp.dot(table, held[part], preferred_element_type=jnp.float32)
        for piece in range(PART // LANES):
            blocks[part * (PART // LANES) + piece] = product[
                :, piece * LANES : (piece + 1) * LANES
            ]
    for out, other in ((send, core ^ 1), (keep, core)):
        for b in range(2):
            for c in range(2):
                out[b, c, :IN_SENT] = blocks[(y ^ b ^ (3 * c)) * 2 + other]
    send[:, :, IN_SENT:] = jnp.zeros((2, 2, SENT_ROWS - IN_SENT, LANES), jnp.float32)


def output_kernel(table, grads, send, keep):
    x = lax.axis_index("x")
    for b, out in ((1, send), (0, keep)):
        for c in range(2):
            out[c] = jnp.dot(
                table[...], grads[x ^ b ^ (3 * c)], preferred_element_type=jnp.float32
            )


def add_kernel(own, got, after, send, keep):
    keep[...] = own[0] + got[0]
    send[...] = own[1] + got[1]


def add_core_kernel(own, got, send, keep):
    keep[...] = own[0] + got[0, :, :IN_SENT]
    send[...] = own[1] + got[1, :, :IN_SENT]


def pack_kernel(in_own, in_got, out_own, out_got, packed):
    side_in = in_own[...] + in_got[...]
    side_out = out_own[...] + out_got[...]
    for dest in range(8):
        half = (dest // 4) * OUT_HERE
        packed[dest, :OUT_HERE] = side_out[half : half + OUT_HERE]
        half = (dest % 2) * IN_HERE
        packed[dest, OUT_HERE:] = side_in[half : half + IN_HERE]


def feature_kernel(packed, spread):
    factor_half = lax.shift_right_logical(lax.axis_index("zl"), 1)
    sides_in, sides_out = [], []
    for z in range(2):
        source = z * 4
        sides_out.append(
            (packed[source, :OUT_HERE] + packed[source + 1, :OUT_HERE])
            + (packed[source + 2, :OUT_HERE] + packed[source + 3, :OUT_HERE])
        )
        source = z * 2 + factor_half
        sides_in.append(packed[source, OUT_HERE:] + packed[4 + source, OUT_HERE:])
    product = lax.dot_general(
        jnp.concatenate(sides_in, axis=1) * SEQ_LEN ** (-0.5),
        jnp.concatenate(sides_out, axis=1),
        (((1,), (1,)), ((), ())),
        precision=lax.Precision.HIGHEST,
        preferred_element_type=jnp.float32,
    )
    total = jnp.concatenate(
        [product, jnp.zeros((IN_HERE, LANES - OUT_HERE), jnp.float32)], axis=1
    )
    for place in range(8):
        spread[place] = total if place == 0 else pltpu.roll(total, LANES - 4 * place, 1)


def sum_kernel(parts, features):
    total = parts[0]
    for place in range(1, 8):
        total = total + parts[place]
    for seq in range(SEQS):
        features[seq] = total[2 * seq : 2 * seq + 2, :4]


def body(activations, out_grads, hash_seeds, offsets):
    acts = jnp.swapaxes(activations, 1, 2)
    grads = jnp.swapaxes(out_grads, 1, 2)
    here_in = acts.shape[1]
    vmem = pl.BlockSpec(memory_space=pltpu.VMEM)
    hbm = pl.BlockSpec(memory_space=pltpu.HBM)
    anywhere = pl.BlockSpec(memory_space=pl.ANY)
    params = pltpu.CompilerParams(vmem_limit_bytes=16 * 1024 * 1024)

    def shaped(*dims):
        return jax.ShapeDtypeStruct(dims, jnp.float32)

    def pinned(value):
        return pltpu.with_memory_space_constraint(value, pltpu.HBM)

    def swap(value, axis, distance):
        size = SIZES[AXES.index(axis)]
        return lax.ppermute(value, axis, [(i, i ^ distance) for i in range(size)])

    def add(own, got, after, name):
        return pl.pallas_call(
            add_kernel,
            out_shape=[shaped(*own.shape[1:])] * 2,
            in_specs=[vmem, vmem, anywhere],
            out_specs=[vmem] * 2,
            compiler_params=params,
            name=name,
        )(own, got, after)

    in_send, in_keep, out_table = pl.pallas_call(
        input_kernel,
        out_shape=[shaped(2, 2, SENT_ROWS, LANES), shaped(2, 2, IN_SENT, LANES)]
        + [jax.ShapeDtypeStruct((K_OUT, grads.shape[1]), jnp.bfloat16)],
        in_specs=[hbm] * 3,
        out_specs=[vmem] * 3,
        scratch_shapes=[
            pltpu.SMEM((2,), jnp.int32),
            pltpu.SMEM((2,), jnp.int32),
            pltpu.VMEM((PARTS, here_in, PART), jnp.bfloat16),
            pltpu.VMEM((BLOCKS // 2, IN_SENT, LANES), jnp.float32),
            pltpu.SemaphoreType.DMA((PARTS,)),
            pltpu.SemaphoreType.DMA((2,)),
        ],
        compiler_params=params,
        name="input_terms",
    )(pinned(hash_seeds), pinned(offsets), pinned(acts))
    in_got = swap(in_send, "core", 1)
    out_send, out_keep = pl.pallas_call(
        output_kernel,
        out_shape=[shaped(2, K_OUT, LANES)] * 2,
        in_specs=[vmem] * 2,
        out_specs=[vmem] * 2,
        compiler_params=params,
        name="output_terms",
    )(out_table, grads)
    in_send, in_keep = pl.pallas_call(
        add_core_kernel,
        out_shape=[shaped(2, IN_SENT, LANES)] * 2,
        in_specs=[vmem] * 2,
        out_specs=[vmem] * 2,
        compiler_params=params,
        name="add_core",
    )(in_keep, in_got)
    in_got = swap(in_send, "y", 1)
    out_got = swap(out_send, "x", 1)
    in_send, in_keep = add(in_keep, in_got, in_got, "add_y")
    in_got = swap(in_send, "y", 3)
    out_send, out_keep = add(out_keep, out_got, in_send, "add_x")
    out_got = swap(out_send, "x", 3)
    packed = pl.pallas_call(
        pack_kernel,
        out_shape=shaped(8, OUT_HERE + IN_HERE, LANES),
        in_specs=[vmem] * 4,
        out_specs=vmem,
        compiler_params=params,
        name="pack_sides",
    )(in_keep, in_got, out_keep, out_got)
    packed = lax.all_to_all(packed, ("zh", "zl"), 0, 0, tiled=True)
    spread = pl.pallas_call(
        feature_kernel,
        out_shape=shaped(8, 8, LANES),
        in_specs=[vmem],
        out_specs=vmem,
        compiler_params=params,
        name="feature_partials",
    )(packed)
    spread = lax.all_to_all(
        spread.reshape(32, 2, LANES), ("y", "core", "x"), 0, 0, tiled=True
    )
    summed = jnp.sum(spread.reshape(8, SEQS, 2, LANES), axis=0)
    return summed[:, :, :4]


def solution(mesh):
    fine = Mesh(mesh.devices.reshape(SIZES), AXES)
    return jax.shard_map(
        body,
        mesh=fine,
        in_specs=(P(None, None, ROW), P(None, ROW, COL), P(), P()),
        out_specs=P(None, COL, ROW),
        check_vma=False,
    )
```

```python
import jax
import jax.numpy as jnp
from jax import lax
from jax.experimental import pallas as pl
from jax.experimental.pallas import tpu as pltpu
from jax.sharding import Mesh, PartitionSpec as P

D = 5120
FF = 13824
K_IN = 32
K_OUT = 64
SEQ_LEN = 2048
SEQS = 4
LANES = 128
BLOCKS = SEQ_LEN // LANES
IN_HERE = 8
IN_SENT = 16
SENT_ROWS = 40
PADDED_ROWS = 36
PARTS = 2
PART = SEQ_LEN // 2 // PARTS
OUT_HERE = 32
MULTIPLIER = 73244475
AXES = ("zh", "y", "core", "zl", "x")
SIZES = (2, 4, 2, 4, 4)
ROW = ("zh", "y", "core")
COL = ("zl", "x")

SIN_TURN = (
    6.283185280154403,
    -41.34168061334532,
    81.60247636883796,
    -76.5811726421402,
    39.75982706857711,
)


def scramble(counter, seed_value):
    hashed = counter ^ seed_value
    hashed = hashed * jnp.int32(MULTIPLIER)
    hashed = hashed ^ lax.shift_right_logical(hashed, jnp.full_like(hashed, 16))
    hashed = hashed * jnp.int32(MULTIPLIER)
    return hashed ^ lax.shift_right_logical(hashed, jnp.full_like(hashed, 16))


def unit_draw(hashed):
    top_bits = lax.shift_right_logical(hashed, jnp.full_like(hashed, 8))
    return (top_bits.astype(jnp.float32) + 0.5) * (1.0 / 16777216.0)


def cos_turn(angle):
    quarter = jnp.abs(angle - 0.5) - 0.25
    square = quarter * quarter
    total = jnp.full_like(square, SIN_TURN[-1])
    for term in SIN_TURN[-2::-1]:
        total = total * square + term
    return total * quarter


def normal_draw(counter, seed_value, fan_in):
    radius = jnp.sqrt(-2.0 * jnp.log(unit_draw(scramble(2 * counter, seed_value))))
    angle = unit_draw(scramble(2 * counter + 1, seed_value))
    return (radius * cos_turn(angle) * fan_in ** (-0.5)).astype(jnp.bfloat16)


def input_kernel(
    seeds_hbm, offsets_hbm, acts, send, keep, out_table, seeds, offsets, held, blocks, arrived, told
):
    zh, y, core, zl, x = (lax.axis_index(axis) for axis in AXES)
    here = acts.shape[1]
    half = lax.shift_right_logical(zl, 1)
    tell = [
        pltpu.make_async_copy(seeds_hbm, seeds, told.at[0]),
        pltpu.make_async_copy(offsets_hbm, offsets, told.at[1]),
    ]
    for copy in tell:
        copy.start()
    fetches = []
    for part in range(PARTS):
        start = pl.multiple_of(half * (SEQ_LEN // 2) + part * PART, PART)
        fetch = pltpu.make_async_copy(
            acts.at[x, :, pl.ds(start, PART)], held.at[part], arrived.at[part]
        )
        fetch.start()
        fetches.append(fetch)
    for copy in tell:
        copy.wait()
    shape = (IN_SENT, here)
    factor = (zl & 1) * IN_SENT + lax.broadcasted_iota(jnp.int32, shape, 0)
    row = (zh * 4 + y) * 2 + core
    feature = row * here + lax.broadcasted_iota(jnp.int32, shape, 1)
    table = normal_draw(offsets[0] + feature * K_IN + factor, seeds[0], D)
    shape = out_table.shape
    factor = lax.broadcasted_iota(jnp.int32, shape, 0)
    feature = (zl * 4 + x) * shape[1] + lax.broadcasted_iota(jnp.int32, shape, 1)
    out_table[...] = normal_draw(offsets[1] + feature * K_OUT + factor, seeds[1], FF)
    for part in range(PARTS):
        fetches[part].wait()
        product = jnp.dot(table, held[part], preferred_element_type=jnp.float32)
        for piece in range(PART // LANES):
            blocks[part * (PART // LANES) + piece] = product[
                :, piece * LANES : (piece + 1) * LANES
            ]
    for out, other in ((send, core ^ 1), (keep, core)):
        for b in range(2):
            for c in range(2):
                out[b, c, :IN_SENT] = blocks[(y ^ (3 * b) ^ c) * 2 + other]
    send[:, :, IN_SENT:] = jnp.zeros((2, 2, SENT_ROWS - IN_SENT, LANES), jnp.float32)


def output_kernel(table, grads, send, keep):
    x = lax.axis_index("x")
    for b, out in ((1, send), (0, keep)):
        for c in range(2):
            out[c] = jnp.dot(
                table[...], grads[x ^ b ^ (3 * c)], preferred_element_type=jnp.float32
            )


def add_kernel(own, got, after, send, keep):
    keep[...] = own[0] + got[0]
    send[...] = own[1] + got[1]


def add_core_kernel(own, got, send, keep):
    keep[...] = own[0] + got[0, :, :IN_SENT]
    send[:, :IN_SENT] = own[1] + got[1, :, :IN_SENT]
    send[:, IN_SENT:] = jnp.zeros((2, PADDED_ROWS - IN_SENT, LANES), jnp.float32)


def add_y_kernel(own, got, after, send, keep):
    keep[...] = own[0] + got[0, :IN_SENT]
    send[...] = own[1] + got[1, :IN_SENT]


def pack_kernel(in_own, in_got, out_own, out_got, packed):
    side_in = in_own[...] + in_got[...]
    side_out = out_own[...] + out_got[...]
    for dest in range(8):
        half = (dest // 4) * OUT_HERE
        packed[dest, :OUT_HERE] = side_out[half : half + OUT_HERE]
        half = (dest % 2) * IN_HERE
        packed[dest, OUT_HERE:] = side_in[half : half + IN_HERE]


def feature_kernel(packed, spread):
    factor_half = lax.shift_right_logical(lax.axis_index("zl"), 1)
    sides_in, sides_out = [], []
    for z in range(2):
        source = z * 4
        sides_out.append(
            (packed[source, :OUT_HERE] + packed[source + 1, :OUT_HERE])
            + (packed[source + 2, :OUT_HERE] + packed[source + 3, :OUT_HERE])
        )
        source = z * 2 + factor_half
        sides_in.append(packed[source, OUT_HERE:] + packed[4 + source, OUT_HERE:])
    product = lax.dot_general(
        jnp.concatenate(sides_in, axis=1) * SEQ_LEN ** (-0.5),
        jnp.concatenate(sides_out, axis=1),
        (((1,), (1,)), ((), ())),
        precision=lax.Precision.HIGHEST,
        preferred_element_type=jnp.float32,
    )
    total = jnp.concatenate(
        [product, jnp.zeros((IN_HERE, LANES - OUT_HERE), jnp.float32)], axis=1
    )
    for place in range(8):
        spread[place] = total if place == 0 else pltpu.roll(total, LANES - 4 * place, 1)


def sum_kernel(parts, features):
    total = parts[0]
    for place in range(1, 8):
        total = total + parts[place]
    for seq in range(SEQS):
        features[seq] = total[2 * seq : 2 * seq + 2, :4]


def body(activations, out_grads, hash_seeds, offsets):
    acts = jnp.swapaxes(activations, 1, 2)
    grads = jnp.swapaxes(out_grads, 1, 2)
    here_in = acts.shape[1]
    vmem = pl.BlockSpec(memory_space=pltpu.VMEM)
    hbm = pl.BlockSpec(memory_space=pltpu.HBM)
    anywhere = pl.BlockSpec(memory_space=pl.ANY)
    params = pltpu.CompilerParams(vmem_limit_bytes=16 * 1024 * 1024)

    def shaped(*dims):
        return jax.ShapeDtypeStruct(dims, jnp.float32)

    def pinned(value):
        return pltpu.with_memory_space_constraint(value, pltpu.HBM)

    def swap(value, axis, distance):
        size = SIZES[AXES.index(axis)]
        return lax.ppermute(value, axis, [(i, i ^ distance) for i in range(size)])

    def add(own, got, after, name):
        return pl.pallas_call(
            add_kernel,
            out_shape=[shaped(*own.shape[1:])] * 2,
            in_specs=[vmem, vmem, anywhere],
            out_specs=[vmem] * 2,
            compiler_params=params,
            name=name,
        )(own, got, after)

    in_send, in_keep, out_table = pl.pallas_call(
        input_kernel,
        out_shape=[shaped(2, 2, SENT_ROWS, LANES), shaped(2, 2, IN_SENT, LANES)]
        + [jax.ShapeDtypeStruct((K_OUT, grads.shape[1]), jnp.bfloat16)],
        in_specs=[hbm] * 3,
        out_specs=[vmem] * 3,
        scratch_shapes=[
            pltpu.SMEM((2,), jnp.int32),
            pltpu.SMEM((2,), jnp.int32),
            pltpu.VMEM((PARTS, here_in, PART), jnp.bfloat16),
            pltpu.VMEM((BLOCKS // 2, IN_SENT, LANES), jnp.float32),
            pltpu.SemaphoreType.DMA((PARTS,)),
            pltpu.SemaphoreType.DMA((2,)),
        ],
        compiler_params=params,
        name="input_terms",
    )(pinned(hash_seeds), pinned(offsets), pinned(acts))
    in_got = swap(in_send, "core", 1)
    out_send, out_keep = pl.pallas_call(
        output_kernel,
        out_shape=[shaped(2, K_OUT, LANES)] * 2,
        in_specs=[vmem] * 2,
        out_specs=[vmem] * 2,
        compiler_params=params,
        name="output_terms",
    )(out_table, grads)
    in_send, in_keep = pl.pallas_call(
        add_core_kernel,
        out_shape=[shaped(2, PADDED_ROWS, LANES), shaped(2, IN_SENT, LANES)],
        in_specs=[vmem] * 2,
        out_specs=[vmem] * 2,
        compiler_params=params,
        name="add_core",
    )(in_keep, in_got)
    in_got = swap(in_send, "y", 3)
    out_got = swap(out_send, "x", 1)
    out_send, out_keep = add(out_keep, out_got, in_send, "add_x")
    out_got = swap(out_send, "x", 3)
    in_send, in_keep = pl.pallas_call(
        add_y_kernel,
        out_shape=[shaped(IN_SENT, LANES)] * 2,
        in_specs=[vmem, vmem, anywhere],
        out_specs=[vmem] * 2,
        compiler_params=params,
        name="add_y",
    )(in_keep, in_got, out_send)
    in_got = swap(in_send, "y", 1)
    packed = pl.pallas_call(
        pack_kernel,
        out_shape=shaped(8, OUT_HERE + IN_HERE, LANES),
        in_specs=[vmem] * 4,
        out_specs=vmem,
        compiler_params=params,
        name="pack_sides",
    )(in_keep, in_got, out_keep, out_got)
    packed = lax.all_to_all(packed, ("zh", "zl"), 0, 0, tiled=True)
    spread = pl.pallas_call(
        feature_kernel,
        out_shape=shaped(8, 8, LANES),
        in_specs=[vmem],
        out_specs=vmem,
        compiler_params=params,
        name="feature_partials",
    )(packed)
    spread = lax.all_to_all(
        spread.reshape(32, 2, LANES), ("y", "core", "x"), 0, 0, tiled=True
    )
    summed = jnp.sum(spread.reshape(8, SEQS, 2, LANES), axis=0)
    return summed[:, :, :4]


def solution(mesh):
    fine = Mesh(mesh.devices.reshape(SIZES), AXES)
    return jax.shard_map(
        body,
        mesh=fine,
        in_specs=(P(None, None, ROW), P(None, ROW, COL), P(), P()),
        out_specs=P(None, COL, ROW),
        check_vma=False,
    )
```

```python
import jax
import jax.numpy as jnp
from jax import lax
from jax.experimental import pallas as pl
from jax.experimental.pallas import tpu as pltpu
from jax.sharding import Mesh, PartitionSpec as P

D = 5120
FF = 13824
K_IN = 32
K_OUT = 64
SEQ_LEN = 2048
SEQS = 4
LANES = 128
BLOCKS = SEQ_LEN // LANES
IN_HERE = 8
IN_SENT = 16
SENT_ROWS = 40
PADDED_ROWS = 36
PARTS = 2
PART = SEQ_LEN // 2 // PARTS
OUT_HERE = 32
MULTIPLIER = 73244475
AXES = ("zh", "y", "core", "zl", "x")
SIZES = (2, 4, 2, 4, 4)
ROW = ("zh", "y", "core")
COL = ("zl", "x")

SIN_TURN = (
    6.283185280154403,
    -41.34168061334532,
    81.60247636883796,
    -76.5811726421402,
    39.75982706857711,
)


def scramble(counter, seed_value):
    hashed = counter ^ seed_value
    hashed = hashed * jnp.int32(MULTIPLIER)
    hashed = hashed ^ lax.shift_right_logical(hashed, jnp.full_like(hashed, 16))
    hashed = hashed * jnp.int32(MULTIPLIER)
    return hashed ^ lax.shift_right_logical(hashed, jnp.full_like(hashed, 16))


def unit_draw(hashed):
    top_bits = lax.shift_right_logical(hashed, jnp.full_like(hashed, 8))
    return (top_bits.astype(jnp.float32) + 0.5) * (1.0 / 16777216.0)


def cos_turn(angle):
    quarter = jnp.abs(angle - 0.5) - 0.25
    square = quarter * quarter
    total = jnp.full_like(square, SIN_TURN[-1])
    for term in SIN_TURN[-2::-1]:
        total = total * square + term
    return total * quarter


def normal_draw(counter, seed_value, fan_in):
    radius = jnp.sqrt(-2.0 * jnp.log(unit_draw(scramble(2 * counter, seed_value))))
    angle = unit_draw(scramble(2 * counter + 1, seed_value))
    return (radius * cos_turn(angle) * fan_in ** (-0.5)).astype(jnp.bfloat16)


def input_kernel(
    seeds_hbm, offsets_hbm, acts, send, keep, out_table, seeds, offsets, held, blocks, arrived, told
):
    zh, y, core, zl, x = (lax.axis_index(axis) for axis in AXES)
    here = acts.shape[1]
    half = lax.shift_right_logical(zl, 1)
    tell = [
        pltpu.make_async_copy(seeds_hbm, seeds, told.at[0]),
        pltpu.make_async_copy(offsets_hbm, offsets, told.at[1]),
    ]
    for copy in tell:
        copy.start()
    fetches = []
    for part in range(PARTS):
        start = pl.multiple_of(half * (SEQ_LEN // 2) + part * PART, PART)
        fetch = pltpu.make_async_copy(
            acts.at[x, :, pl.ds(start, PART)], held.at[part], arrived.at[part]
        )
        fetch.start()
        fetches.append(fetch)
    for copy in tell:
        copy.wait()
    shape = (IN_SENT, here)
    factor = (zl & 1) * IN_SENT + lax.broadcasted_iota(jnp.int32, shape, 0)
    row = (zh * 4 + y) * 2 + core
    feature = row * here + lax.broadcasted_iota(jnp.int32, shape, 1)
    table = normal_draw(offsets[0] + feature * K_IN + factor, seeds[0], D)
    shape = out_table.shape
    factor = lax.broadcasted_iota(jnp.int32, shape, 0)
    feature = (zl * 4 + x) * shape[1] + lax.broadcasted_iota(jnp.int32, shape, 1)
    out_table[...] = normal_draw(offsets[1] + feature * K_OUT + factor, seeds[1], FF)
    for part in range(PARTS):
        fetches[part].wait()
        product = jnp.dot(table, held[part], preferred_element_type=jnp.float32)
        for piece in range(PART // LANES):
            blocks[part * (PART // LANES) + piece] = product[
                :, piece * LANES : (piece + 1) * LANES
            ]
    for out, other in ((send, core ^ 1), (keep, core)):
        for b in range(2):
            for c in range(2):
                out[b, c, :IN_SENT] = blocks[(y ^ (3 * b) ^ c) * 2 + other]
    send[:, :, IN_SENT:] = jnp.zeros((2, 2, SENT_ROWS - IN_SENT, LANES), jnp.float32)


def output_kernel(table, grads, send, keep):
    x = lax.axis_index("x")
    for b, out in ((1, send), (0, keep)):
        for c in range(2):
            out[c] = jnp.dot(
                table[...], grads[x ^ b ^ (3 * c)], preferred_element_type=jnp.float32
            )


def add_kernel(own, got, after, send, keep):
    keep[...] = own[0] + got[0]
    send[...] = own[1] + got[1]


def add_core_kernel(own, got, send, keep):
    keep[...] = own[0] + got[0, :, :IN_SENT]
    send[:, :IN_SENT] = own[1] + got[1, :, :IN_SENT]
    send[:, IN_SENT:] = jnp.zeros((2, PADDED_ROWS - IN_SENT, LANES), jnp.float32)


def add_y_kernel(own, got, after, send, keep):
    keep[...] = own[0] + got[0, :IN_SENT]
    send[...] = own[1] + got[1, :IN_SENT]


def pack_kernel(in_own, in_got, out_own, out_got, packed):
    side_in = in_own[...] + in_got[...]
    side_out = out_own[...] + out_got[...]
    for dest in range(8):
        half = (dest % 2) * OUT_HERE
        packed[dest, :OUT_HERE] = side_out[half : half + OUT_HERE]
        half = (dest // 2 % 2) * IN_HERE
        packed[dest, OUT_HERE:] = side_in[half : half + IN_HERE]


def feature_kernel(packed, spread):
    factor_half = lax.shift_right_logical(lax.axis_index("zl"), 1)
    sides_in, sides_out = [], []
    for z in range(2):
        sides_out.append(
            (packed[z, :OUT_HERE] + packed[2 + z, :OUT_HERE])
            + (packed[4 + z, :OUT_HERE] + packed[6 + z, :OUT_HERE])
        )
        source = (z * 2 + factor_half) * 2
        sides_in.append(packed[source, OUT_HERE:] + packed[source + 1, OUT_HERE:])
    product = lax.dot_general(
        jnp.concatenate(sides_in, axis=1) * SEQ_LEN ** (-0.5),
        jnp.concatenate(sides_out, axis=1),
        (((1,), (1,)), ((), ())),
        precision=lax.Precision.HIGHEST,
        preferred_element_type=jnp.float32,
    )
    total = jnp.concatenate(
        [product, jnp.zeros((IN_HERE, LANES - OUT_HERE), jnp.float32)], axis=1
    )
    for place in range(8):
        spread[place] = total if place == 0 else pltpu.roll(total, LANES - 4 * place, 1)


def sum_kernel(parts, features):
    total = parts[0]
    for place in range(1, 8):
        total = total + parts[place]
    for seq in range(SEQS):
        features[seq] = total[2 * seq : 2 * seq + 2, :4]


def body(activations, out_grads, hash_seeds, offsets):
    acts = jnp.swapaxes(activations, 1, 2)
    grads = jnp.swapaxes(out_grads, 1, 2)
    here_in = acts.shape[1]
    vmem = pl.BlockSpec(memory_space=pltpu.VMEM)
    hbm = pl.BlockSpec(memory_space=pltpu.HBM)
    anywhere = pl.BlockSpec(memory_space=pl.ANY)
    params = pltpu.CompilerParams(vmem_limit_bytes=16 * 1024 * 1024)

    def shaped(*dims):
        return jax.ShapeDtypeStruct(dims, jnp.float32)

    def pinned(value):
        return pltpu.with_memory_space_constraint(value, pltpu.HBM)

    def swap(value, axis, distance):
        size = SIZES[AXES.index(axis)]
        return lax.ppermute(value, axis, [(i, i ^ distance) for i in range(size)])

    def add(own, got, after, name):
        return pl.pallas_call(
            add_kernel,
            out_shape=[shaped(*own.shape[1:])] * 2,
            in_specs=[vmem, vmem, anywhere],
            out_specs=[vmem] * 2,
            compiler_params=params,
            name=name,
        )(own, got, after)

    in_send, in_keep, out_table = pl.pallas_call(
        input_kernel,
        out_shape=[shaped(2, 2, SENT_ROWS, LANES), shaped(2, 2, IN_SENT, LANES)]
        + [jax.ShapeDtypeStruct((K_OUT, grads.shape[1]), jnp.bfloat16)],
        in_specs=[hbm] * 3,
        out_specs=[vmem] * 3,
        scratch_shapes=[
            pltpu.SMEM((2,), jnp.int32),
            pltpu.SMEM((2,), jnp.int32),
            pltpu.VMEM((PARTS, here_in, PART), jnp.bfloat16),
            pltpu.VMEM((BLOCKS // 2, IN_SENT, LANES), jnp.float32),
            pltpu.SemaphoreType.DMA((PARTS,)),
            pltpu.SemaphoreType.DMA((2,)),
        ],
        compiler_params=params,
        name="input_terms",
    )(pinned(hash_seeds), pinned(offsets), pinned(acts))
    in_got = swap(in_send, "core", 1)
    out_send, out_keep = pl.pallas_call(
        output_kernel,
        out_shape=[shaped(2, K_OUT, LANES)] * 2,
        in_specs=[vmem] * 2,
        out_specs=[vmem] * 2,
        compiler_params=params,
        name="output_terms",
    )(out_table, grads)
    in_send, in_keep = pl.pallas_call(
        add_core_kernel,
        out_shape=[shaped(2, PADDED_ROWS, LANES), shaped(2, IN_SENT, LANES)],
        in_specs=[vmem] * 2,
        out_specs=[vmem] * 2,
        compiler_params=params,
        name="add_core",
    )(in_keep, in_got)
    in_got = swap(in_send, "y", 3)
    out_got = swap(out_send, "x", 1)
    out_send, out_keep = add(out_keep, out_got, in_send, "add_x")
    out_got = swap(out_send, "x", 3)
    in_send, in_keep = pl.pallas_call(
        add_y_kernel,
        out_shape=[shaped(IN_SENT, LANES)] * 2,
        in_specs=[vmem, vmem, anywhere],
        out_specs=[vmem] * 2,
        compiler_params=params,
        name="add_y",
    )(in_keep, in_got, out_send)
    in_got = swap(in_send, "y", 1)
    packed = pl.pallas_call(
        pack_kernel,
        out_shape=shaped(8, OUT_HERE + IN_HERE, LANES),
        in_specs=[vmem] * 4,
        out_specs=vmem,
        compiler_params=params,
        name="pack_sides",
    )(in_keep, in_got, out_keep, out_got)
    packed = lax.all_to_all(packed, ("zl", "zh"), 0, 0, tiled=True)
    spread = pl.pallas_call(
        feature_kernel,
        out_shape=shaped(8, 8, LANES),
        in_specs=[vmem],
        out_specs=vmem,
        compiler_params=params,
        name="feature_partials",
    )(packed)
    spread = lax.all_to_all(
        spread.reshape(32, 2, LANES), ("y", "core", "x"), 0, 0, tiled=True
    )
    summed = jnp.sum(spread.reshape(8, SEQS, 2, LANES), axis=0)
    return summed[:, :, :4]


def solution(mesh):
    fine = Mesh(mesh.devices.reshape(SIZES), AXES)
    return jax.shard_map(
        body,
        mesh=fine,
        in_specs=(P(None, None, ROW), P(None, ROW, COL), P(), P()),
        out_specs=P(None, COL, ROW),
        check_vma=False,
    )
```

```python
import jax
import jax.numpy as jnp
from jax import lax
from jax.experimental import pallas as pl
from jax.experimental.pallas import tpu as pltpu
from jax.sharding import Mesh, PartitionSpec as P

D = 5120
FF = 13824
K_IN = 32
K_OUT = 64
SEQ_LEN = 2048
SEQS = 4
LANES = 128
BLOCKS = SEQ_LEN // LANES
IN_HERE = 8
IN_SENT = 16
SENT_ROWS = 40
PADDED_ROWS = 36
PARTS = 2
PART = SEQ_LEN // 2 // PARTS
OUT_HERE = 32
MULTIPLIER = 73244475
AXES = ("zh", "y", "core", "za", "zb", "x")
SIZES = (2, 4, 2, 2, 2, 4)
ROW = ("zh", "y", "core")
COL = ("za", "zb", "x")

SIN_TURN = (
    6.283185280154403,
    -41.34168061334532,
    81.60247636883796,
    -76.5811726421402,
    39.75982706857711,
)


def scramble(counter, seed_value):
    hashed = counter ^ seed_value
    hashed = hashed * jnp.int32(MULTIPLIER)
    hashed = hashed ^ lax.shift_right_logical(hashed, jnp.full_like(hashed, 16))
    hashed = hashed * jnp.int32(MULTIPLIER)
    return hashed ^ lax.shift_right_logical(hashed, jnp.full_like(hashed, 16))


def unit_draw(hashed):
    top_bits = lax.shift_right_logical(hashed, jnp.full_like(hashed, 8))
    return (top_bits.astype(jnp.float32) + 0.5) * (1.0 / 16777216.0)


def cos_turn(angle):
    quarter = jnp.abs(angle - 0.5) - 0.25
    square = quarter * quarter
    total = jnp.full_like(square, SIN_TURN[-1])
    for term in SIN_TURN[-2::-1]:
        total = total * square + term
    return total * quarter


def normal_draw(counter, seed_value, fan_in):
    radius = jnp.sqrt(-2.0 * jnp.log(unit_draw(scramble(2 * counter, seed_value))))
    angle = unit_draw(scramble(2 * counter + 1, seed_value))
    return (radius * cos_turn(angle) * fan_in ** (-0.5)).astype(jnp.bfloat16)


def input_kernel(
    seeds_hbm, offsets_hbm, acts, send, keep, out_table, seeds, offsets, held, blocks, arrived, told
):
    zh, y, core, za, zb, x = (lax.axis_index(axis) for axis in AXES)
    zl = za * 2 + zb
    here = acts.shape[1]
    half = lax.shift_right_logical(zl, 1)
    tell = [
        pltpu.make_async_copy(seeds_hbm, seeds, told.at[0]),
        pltpu.make_async_copy(offsets_hbm, offsets, told.at[1]),
    ]
    for copy in tell:
        copy.start()
    fetches = []
    for part in range(PARTS):
        start = pl.multiple_of(half * (SEQ_LEN // 2) + part * PART, PART)
        fetch = pltpu.make_async_copy(
            acts.at[x, :, pl.ds(start, PART)], held.at[part], arrived.at[part]
        )
        fetch.start()
        fetches.append(fetch)
    for copy in tell:
        copy.wait()
    shape = (IN_SENT, here)
    factor = (zl & 1) * IN_SENT + lax.broadcasted_iota(jnp.int32, shape, 0)
    row = (zh * 4 + y) * 2 + core
    feature = row * here + lax.broadcasted_iota(jnp.int32, shape, 1)
    table = normal_draw(offsets[0] + feature * K_IN + factor, seeds[0], D)
    shape = out_table.shape
    factor = lax.broadcasted_iota(jnp.int32, shape, 0)
    feature = (zl * 4 + x) * shape[1] + lax.broadcasted_iota(jnp.int32, shape, 1)
    out_table[...] = normal_draw(offsets[1] + feature * K_OUT + factor, seeds[1], FF)
    for part in range(PARTS):
        fetches[part].wait()
        product = jnp.dot(table, held[part], preferred_element_type=jnp.float32)
        for piece in range(PART // LANES):
            blocks[part * (PART // LANES) + piece] = product[
                :, piece * LANES : (piece + 1) * LANES
            ]
    for out, other in ((send, core ^ 1), (keep, core)):
        for b in range(2):
            for c in range(2):
                out[b, c, :IN_SENT] = blocks[(y ^ (3 * b) ^ c) * 2 + other]
    send[:, :, IN_SENT:] = jnp.zeros((2, 2, SENT_ROWS - IN_SENT, LANES), jnp.float32)


def output_kernel(table, grads, send, keep):
    x = lax.axis_index("x")
    for b, out in ((1, send), (0, keep)):
        for c in range(2):
            out[c] = jnp.dot(
                table[...], grads[x ^ b ^ (3 * c)], preferred_element_type=jnp.float32
            )


def add_kernel(own, got, after, send, keep):
    keep[...] = own[0] + got[0]
    send[...] = own[1] + got[1]


def add_core_kernel(own, got, send, keep):
    keep[...] = own[0] + got[0, :, :IN_SENT]
    send[:, :IN_SENT] = own[1] + got[1, :, :IN_SENT]
    send[:, IN_SENT:] = jnp.zeros((2, PADDED_ROWS - IN_SENT, LANES), jnp.float32)


def add_y_kernel(own, got, after, send, keep):
    keep[...] = own[0] + got[0, :IN_SENT]
    send[...] = own[1] + got[1, :IN_SENT]


def pack_kernel(in_own, in_got, out_own, out_got, packed):
    side_in = in_own[...] + in_got[...]
    side_out = out_own[...] + out_got[...]
    for dest in range(8):
        half = (dest % 2) * OUT_HERE
        packed[dest, :OUT_HERE] = side_out[half : half + OUT_HERE]
        half = (dest // 4) * IN_HERE
        packed[dest, OUT_HERE:] = side_in[half : half + IN_HERE]


def feature_kernel(packed, spread):
    factor_half = lax.axis_index("za")
    sides_in, sides_out = [], []
    for z in range(2):
        sides_out.append(
            (packed[z, :OUT_HERE] + packed[2 + z, :OUT_HERE])
            + (packed[4 + z, :OUT_HERE] + packed[6 + z, :OUT_HERE])
        )
        source = factor_half * 4 + z * 2
        sides_in.append(packed[source, OUT_HERE:] + packed[source + 1, OUT_HERE:])
    product = lax.dot_general(
        jnp.concatenate(sides_in, axis=1) * SEQ_LEN ** (-0.5),
        jnp.concatenate(sides_out, axis=1),
        (((1,), (1,)), ((), ())),
        precision=lax.Precision.HIGHEST,
        preferred_element_type=jnp.float32,
    )
    total = jnp.concatenate(
        [product, jnp.zeros((IN_HERE, LANES - OUT_HERE), jnp.float32)], axis=1
    )
    for place in range(8):
        moved = total if place == 0 else pltpu.roll(total, LANES - 4 * place, 1)
        spread[place % 2 * 4 + place // 2] = moved


def sum_kernel(parts, features):
    total = parts[0]
    for place in range(1, 8):
        total = total + parts[place]
    for seq in range(SEQS):
        features[seq] = total[2 * seq : 2 * seq + 2, :4]


def body(activations, out_grads, hash_seeds, offsets):
    acts = jnp.swapaxes(activations, 1, 2)
    grads = jnp.swapaxes(out_grads, 1, 2)
    here_in = acts.shape[1]
    vmem = pl.BlockSpec(memory_space=pltpu.VMEM)
    hbm = pl.BlockSpec(memory_space=pltpu.HBM)
    anywhere = pl.BlockSpec(memory_space=pl.ANY)
    params = pltpu.CompilerParams(vmem_limit_bytes=16 * 1024 * 1024)

    def shaped(*dims):
        return jax.ShapeDtypeStruct(dims, jnp.float32)

    def pinned(value):
        return pltpu.with_memory_space_constraint(value, pltpu.HBM)

    def swap(value, axis, distance):
        size = SIZES[AXES.index(axis)]
        return lax.ppermute(value, axis, [(i, i ^ distance) for i in range(size)])

    def add(own, got, after, name):
        return pl.pallas_call(
            add_kernel,
            out_shape=[shaped(*own.shape[1:])] * 2,
            in_specs=[vmem, vmem, anywhere],
            out_specs=[vmem] * 2,
            compiler_params=params,
            name=name,
        )(own, got, after)

    in_send, in_keep, out_table = pl.pallas_call(
        input_kernel,
        out_shape=[shaped(2, 2, SENT_ROWS, LANES), shaped(2, 2, IN_SENT, LANES)]
        + [jax.ShapeDtypeStruct((K_OUT, grads.shape[1]), jnp.bfloat16)],
        in_specs=[hbm] * 3,
        out_specs=[vmem] * 3,
        scratch_shapes=[
            pltpu.SMEM((2,), jnp.int32),
            pltpu.SMEM((2,), jnp.int32),
            pltpu.VMEM((PARTS, here_in, PART), jnp.bfloat16),
            pltpu.VMEM((BLOCKS // 2, IN_SENT, LANES), jnp.float32),
            pltpu.SemaphoreType.DMA((PARTS,)),
            pltpu.SemaphoreType.DMA((2,)),
        ],
        compiler_params=params,
        name="input_terms",
    )(pinned(hash_seeds), pinned(offsets), pinned(acts))
    in_got = swap(in_send, "core", 1)
    out_send, out_keep = pl.pallas_call(
        output_kernel,
        out_shape=[shaped(2, K_OUT, LANES)] * 2,
        in_specs=[vmem] * 2,
        out_specs=[vmem] * 2,
        compiler_params=params,
        name="output_terms",
    )(out_table, grads)
    in_send, in_keep = pl.pallas_call(
        add_core_kernel,
        out_shape=[shaped(2, PADDED_ROWS, LANES), shaped(2, IN_SENT, LANES)],
        in_specs=[vmem] * 2,
        out_specs=[vmem] * 2,
        compiler_params=params,
        name="add_core",
    )(in_keep, in_got)
    in_got = swap(in_send, "y", 3)
    out_got = swap(out_send, "x", 1)
    out_send, out_keep = add(out_keep, out_got, in_send, "add_x")
    out_got = swap(out_send, "x", 3)
    in_send, in_keep = pl.pallas_call(
        add_y_kernel,
        out_shape=[shaped(IN_SENT, LANES)] * 2,
        in_specs=[vmem, vmem, anywhere],
        out_specs=[vmem] * 2,
        compiler_params=params,
        name="add_y",
    )(in_keep, in_got, out_send)
    in_got = swap(in_send, "y", 1)
    packed = pl.pallas_call(
        pack_kernel,
        out_shape=shaped(8, OUT_HERE + IN_HERE, LANES),
        in_specs=[vmem] * 4,
        out_specs=vmem,
        compiler_params=params,
        name="pack_sides",
    )(in_keep, in_got, out_keep, out_got)
    packed = lax.all_to_all(packed, ("zb", "za", "zh"), 0, 0, tiled=True)
    spread = pl.pallas_call(
        feature_kernel,
        out_shape=shaped(8, 8, LANES),
        in_specs=[vmem],
        out_specs=vmem,
        compiler_params=params,
        name="feature_partials",
    )(packed)
    spread = lax.all_to_all(
        spread.reshape(32, 2, LANES), ("core", "y", "x"), 0, 0, tiled=True
    )
    summed = jnp.sum(spread.reshape(8, SEQS, 2, LANES), axis=0)
    return summed[:, :, :4]


def solution(mesh):
    fine = Mesh(mesh.devices.reshape(SIZES), AXES)
    return jax.shard_map(
        body,
        mesh=fine,
        in_specs=(P(None, None, ROW), P(None, ROW, COL), P(), P()),
        out_specs=P(None, COL, ROW),
        check_vma=False,
    )
```

```python
import jax
import jax.numpy as jnp
from jax import lax
from jax.experimental import pallas as pl
from jax.experimental.pallas import tpu as pltpu
from jax.sharding import Mesh, PartitionSpec as P

D = 5120
FF = 13824
K_IN = 32
K_OUT = 64
SEQ_LEN = 2048
SEQS = 4
LANES = 128
BLOCKS = SEQ_LEN // LANES
IN_HERE = 8
IN_SENT = 16
SENT_ROWS = 40
PADDED_ROWS = 36
PARTS = 1
PART = SEQ_LEN // 2 // PARTS
OUT_HERE = 32
MULTIPLIER = 73244475
AXES = ("zh", "y", "core", "za", "zb", "x")
SIZES = (2, 4, 2, 2, 2, 4)
ROW = ("zh", "y", "core")
COL = ("za", "zb", "x")

SIN_TURN = (
    6.283185280154403,
    -41.34168061334532,
    81.60247636883796,
    -76.5811726421402,
    39.75982706857711,
)


def scramble(counter, seed_value):
    hashed = counter ^ seed_value
    hashed = hashed * jnp.int32(MULTIPLIER)
    hashed = hashed ^ lax.shift_right_logical(hashed, jnp.full_like(hashed, 16))
    hashed = hashed * jnp.int32(MULTIPLIER)
    return hashed ^ lax.shift_right_logical(hashed, jnp.full_like(hashed, 16))


def unit_draw(hashed):
    top_bits = lax.shift_right_logical(hashed, jnp.full_like(hashed, 8))
    return (top_bits.astype(jnp.float32) + 0.5) * (1.0 / 16777216.0)


def cos_turn(angle):
    quarter = jnp.abs(angle - 0.5) - 0.25
    square = quarter * quarter
    total = jnp.full_like(square, SIN_TURN[-1])
    for term in SIN_TURN[-2::-1]:
        total = total * square + term
    return total * quarter


def normal_draw(counter, seed_value, fan_in):
    radius = jnp.sqrt(-2.0 * jnp.log(unit_draw(scramble(2 * counter, seed_value))))
    angle = unit_draw(scramble(2 * counter + 1, seed_value))
    return (radius * cos_turn(angle) * fan_in ** (-0.5)).astype(jnp.bfloat16)


def input_kernel(
    seeds_hbm, offsets_hbm, acts, send, keep, out_table, seeds, offsets, held, blocks, arrived, told
):
    zh, y, core, za, zb, x = (lax.axis_index(axis) for axis in AXES)
    zl = za * 2 + zb
    here = acts.shape[1]
    half = lax.shift_right_logical(zl, 1)
    tell = [
        pltpu.make_async_copy(seeds_hbm, seeds, told.at[0]),
        pltpu.make_async_copy(offsets_hbm, offsets, told.at[1]),
    ]
    for copy in tell:
        copy.start()
    fetches = []
    for part in range(PARTS):
        start = pl.multiple_of(half * (SEQ_LEN // 2) + part * PART, PART)
        fetch = pltpu.make_async_copy(
            acts.at[x, :, pl.ds(start, PART)], held.at[part], arrived.at[part]
        )
        fetch.start()
        fetches.append(fetch)
    for copy in tell:
        copy.wait()
    shape = (IN_SENT, here)
    factor = (zl & 1) * IN_SENT + lax.broadcasted_iota(jnp.int32, shape, 0)
    row = (zh * 4 + y) * 2 + core
    feature = row * here + lax.broadcasted_iota(jnp.int32, shape, 1)
    table = normal_draw(offsets[0] + feature * K_IN + factor, seeds[0], D)
    shape = out_table.shape
    factor = lax.broadcasted_iota(jnp.int32, shape, 0)
    feature = (zl * 4 + x) * shape[1] + lax.broadcasted_iota(jnp.int32, shape, 1)
    out_table[...] = normal_draw(offsets[1] + feature * K_OUT + factor, seeds[1], FF)
    for part in range(PARTS):
        fetches[part].wait()
        product = jnp.dot(table, held[part], preferred_element_type=jnp.float32)
        for piece in range(PART // LANES):
            blocks[part * (PART // LANES) + piece] = product[
                :, piece * LANES : (piece + 1) * LANES
            ]
    for out, other in ((send, core ^ 1), (keep, core)):
        for b in range(2):
            for c in range(2):
                out[b, c, :IN_SENT] = blocks[(y ^ (3 * b) ^ c) * 2 + other]
    send[:, :, IN_SENT:] = jnp.zeros((2, 2, SENT_ROWS - IN_SENT, LANES), jnp.float32)


def output_kernel(table, grads, send, keep):
    x = lax.axis_index("x")
    for b, out in ((1, send), (0, keep)):
        for c in range(2):
            out[c] = jnp.dot(
                table[...], grads[x ^ b ^ (3 * c)], preferred_element_type=jnp.float32
            )


def add_kernel(own, got, after, send, keep):
    keep[...] = own[0] + got[0]
    send[...] = own[1] + got[1]


def add_core_kernel(own, got, send, keep):
    keep[...] = own[0] + got[0, :, :IN_SENT]
    send[:, :IN_SENT] = own[1] + got[1, :, :IN_SENT]
    send[:, IN_SENT:] = jnp.zeros((2, PADDED_ROWS - IN_SENT, LANES), jnp.float32)


def add_y_kernel(own, got, after, send, keep):
    keep[...] = own[0] + got[0, :IN_SENT]
    send[...] = own[1] + got[1, :IN_SENT]


def pack_kernel(in_own, in_got, out_own, out_got, packed):
    side_in = in_own[...] + in_got[...]
    side_out = out_own[...] + out_got[...]
    for dest in range(8):
        half = (dest % 2) * OUT_HERE
        packed[dest, :OUT_HERE] = side_out[half : half + OUT_HERE]
        half = (dest // 4) * IN_HERE
        packed[dest, OUT_HERE:] = side_in[half : half + IN_HERE]


def feature_kernel(packed, spread):
    factor_half = lax.axis_index("za")
    sides_in, sides_out = [], []
    for z in range(2):
        sides_out.append(
            (packed[z, :OUT_HERE] + packed[2 + z, :OUT_HERE])
            + (packed[4 + z, :OUT_HERE] + packed[6 + z, :OUT_HERE])
        )
        source = factor_half * 4 + z * 2
        sides_in.append(packed[source, OUT_HERE:] + packed[source + 1, OUT_HERE:])
    product = lax.dot_general(
        jnp.concatenate(sides_in, axis=1) * SEQ_LEN ** (-0.5),
        jnp.concatenate(sides_out, axis=1),
        (((1,), (1,)), ((), ())),
        precision=lax.Precision.HIGHEST,
        preferred_element_type=jnp.float32,
    )
    total = jnp.concatenate(
        [product, jnp.zeros((IN_HERE, LANES - OUT_HERE), jnp.float32)], axis=1
    )
    for place in range(8):
        moved = total if place == 0 else pltpu.roll(total, LANES - 4 * place, 1)
        spread[place % 2 * 4 + place // 2] = moved


def sum_kernel(parts, features):
    total = parts[0]
    for place in range(1, 8):
        total = total + parts[place]
    for seq in range(SEQS):
        features[seq] = total[2 * seq : 2 * seq + 2, :4]


def body(activations, out_grads, hash_seeds, offsets):
    acts = jnp.swapaxes(activations, 1, 2)
    grads = jnp.swapaxes(out_grads, 1, 2)
    here_in = acts.shape[1]
    vmem = pl.BlockSpec(memory_space=pltpu.VMEM)
    hbm = pl.BlockSpec(memory_space=pltpu.HBM)
    anywhere = pl.BlockSpec(memory_space=pl.ANY)
    params = pltpu.CompilerParams(vmem_limit_bytes=16 * 1024 * 1024)

    def shaped(*dims):
        return jax.ShapeDtypeStruct(dims, jnp.float32)

    def pinned(value):
        return pltpu.with_memory_space_constraint(value, pltpu.HBM)

    def swap(value, axis, distance):
        size = SIZES[AXES.index(axis)]
        return lax.ppermute(value, axis, [(i, i ^ distance) for i in range(size)])

    def add(own, got, after, name):
        return pl.pallas_call(
            add_kernel,
            out_shape=[shaped(*own.shape[1:])] * 2,
            in_specs=[vmem, vmem, anywhere],
            out_specs=[vmem] * 2,
            compiler_params=params,
            name=name,
        )(own, got, after)

    in_send, in_keep, out_table = pl.pallas_call(
        input_kernel,
        out_shape=[shaped(2, 2, SENT_ROWS, LANES), shaped(2, 2, IN_SENT, LANES)]
        + [jax.ShapeDtypeStruct((K_OUT, grads.shape[1]), jnp.bfloat16)],
        in_specs=[hbm] * 3,
        out_specs=[vmem] * 3,
        scratch_shapes=[
            pltpu.SMEM((2,), jnp.int32),
            pltpu.SMEM((2,), jnp.int32),
            pltpu.VMEM((PARTS, here_in, PART), jnp.bfloat16),
            pltpu.VMEM((BLOCKS // 2, IN_SENT, LANES), jnp.float32),
            pltpu.SemaphoreType.DMA((PARTS,)),
            pltpu.SemaphoreType.DMA((2,)),
        ],
        compiler_params=params,
        name="input_terms",
    )(pinned(hash_seeds), pinned(offsets), pinned(acts))
    in_got = swap(in_send, "core", 1)
    out_send, out_keep = pl.pallas_call(
        output_kernel,
        out_shape=[shaped(2, K_OUT, LANES)] * 2,
        in_specs=[vmem] * 2,
        out_specs=[vmem] * 2,
        compiler_params=params,
        name="output_terms",
    )(out_table, grads)
    in_send, in_keep = pl.pallas_call(
        add_core_kernel,
        out_shape=[shaped(2, PADDED_ROWS, LANES), shaped(2, IN_SENT, LANES)],
        in_specs=[vmem] * 2,
        out_specs=[vmem] * 2,
        compiler_params=params,
        name="add_core",
    )(in_keep, in_got)
    in_got = swap(in_send, "y", 3)
    out_got = swap(out_send, "x", 1)
    out_send, out_keep = add(out_keep, out_got, in_send, "add_x")
    out_got = swap(out_send, "x", 3)
    in_send, in_keep = pl.pallas_call(
        add_y_kernel,
        out_shape=[shaped(IN_SENT, LANES)] * 2,
        in_specs=[vmem, vmem, anywhere],
        out_specs=[vmem] * 2,
        compiler_params=params,
        name="add_y",
    )(in_keep, in_got, out_send)
    in_got = swap(in_send, "y", 1)
    packed = pl.pallas_call(
        pack_kernel,
        out_shape=shaped(8, OUT_HERE + IN_HERE, LANES),
        in_specs=[vmem] * 4,
        out_specs=vmem,
        compiler_params=params,
        name="pack_sides",
    )(in_keep, in_got, out_keep, out_got)
    packed = lax.all_to_all(packed, ("zb", "za", "zh"), 0, 0, tiled=True)
    spread = pl.pallas_call(
        feature_kernel,
        out_shape=shaped(8, 8, LANES),
        in_specs=[vmem],
        out_specs=vmem,
        compiler_params=params,
        name="feature_partials",
    )(packed)
    spread = lax.all_to_all(
        spread.reshape(32, 2, LANES), ("core", "y", "x"), 0, 0, tiled=True
    )
    summed = jnp.sum(spread.reshape(8, SEQS, 2, LANES), axis=0)
    return summed[:, :, :4]


def solution(mesh):
    fine = Mesh(mesh.devices.reshape(SIZES), AXES)
    return jax.shard_map(
        body,
        mesh=fine,
        in_specs=(P(None, None, ROW), P(None, ROW, COL), P(), P()),
        out_specs=P(None, COL, ROW),
        check_vma=False,
    )
```

```python
import jax
import jax.numpy as jnp
from jax import lax
from jax.experimental import pallas as pl
from jax.experimental.pallas import tpu as pltpu
from jax.sharding import Mesh, PartitionSpec as P

D = 5120
FF = 13824
K_IN = 32
K_OUT = 64
SEQ_LEN = 2048
SEQS = 4
LANES = 128
BLOCKS = SEQ_LEN // LANES
IN_HERE = 8
IN_SENT = 16
SENT_ROWS = 36
PADDED_ROWS = 33
PARTS = 1
PART = SEQ_LEN // 2 // PARTS
OUT_HERE = 32
MULTIPLIER = 73244475
AXES = ("zh", "y", "core", "za", "zb", "x")
SIZES = (2, 4, 2, 2, 2, 4)
ROW = ("zh", "y", "core")
COL = ("za", "zb", "x")

SIN_TURN = (
    6.283185280154403,
    -41.34168061334532,
    81.60247636883796,
    -76.5811726421402,
    39.75982706857711,
)


def scramble(counter, seed_value):
    hashed = counter ^ seed_value
    hashed = hashed * jnp.int32(MULTIPLIER)
    hashed = hashed ^ lax.shift_right_logical(hashed, jnp.full_like(hashed, 16))
    hashed = hashed * jnp.int32(MULTIPLIER)
    return hashed ^ lax.shift_right_logical(hashed, jnp.full_like(hashed, 16))


def unit_draw(hashed):
    top_bits = lax.shift_right_logical(hashed, jnp.full_like(hashed, 8))
    return (top_bits.astype(jnp.float32) + 0.5) * (1.0 / 16777216.0)


def cos_turn(angle):
    quarter = jnp.abs(angle - 0.5) - 0.25
    square = quarter * quarter
    total = jnp.full_like(square, SIN_TURN[-1])
    for term in SIN_TURN[-2::-1]:
        total = total * square + term
    return total * quarter


def normal_draw(counter, seed_value, fan_in):
    radius = jnp.sqrt(-2.0 * jnp.log(unit_draw(scramble(2 * counter, seed_value))))
    angle = unit_draw(scramble(2 * counter + 1, seed_value))
    return (radius * cos_turn(angle) * fan_in ** (-0.5)).astype(jnp.bfloat16)


def input_kernel(
    seeds_hbm, offsets_hbm, acts, send, keep, out_table, seeds, offsets, held, blocks, arrived, told
):
    zh, y, core, za, zb, x = (lax.axis_index(axis) for axis in AXES)
    zl = za * 2 + zb
    here = acts.shape[1]
    half = lax.shift_right_logical(zl, 1)
    tell = [
        pltpu.make_async_copy(seeds_hbm, seeds, told.at[0]),
        pltpu.make_async_copy(offsets_hbm, offsets, told.at[1]),
    ]
    for copy in tell:
        copy.start()
    fetches = []
    for part in range(PARTS):
        start = pl.multiple_of(half * (SEQ_LEN // 2) + part * PART, PART)
        fetch = pltpu.make_async_copy(
            acts.at[x, :, pl.ds(start, PART)], held.at[part], arrived.at[part]
        )
        fetch.start()
        fetches.append(fetch)
    for copy in tell:
        copy.wait()
    shape = (IN_SENT, here)
    factor = (zl & 1) * IN_SENT + lax.broadcasted_iota(jnp.int32, shape, 0)
    row = (zh * 4 + y) * 2 + core
    feature = row * here + lax.broadcasted_iota(jnp.int32, shape, 1)
    table = normal_draw(offsets[0] + feature * K_IN + factor, seeds[0], D)
    shape = out_table.shape
    factor = lax.broadcasted_iota(jnp.int32, shape, 0)
    feature = (zl * 4 + x) * shape[1] + lax.broadcasted_iota(jnp.int32, shape, 1)
    out_table[...] = normal_draw(offsets[1] + feature * K_OUT + factor, seeds[1], FF)
    for part in range(PARTS):
        fetches[part].wait()
        product = jnp.dot(table, held[part], preferred_element_type=jnp.float32)
        for piece in range(PART // LANES):
            blocks[part * (PART // LANES) + piece] = product[
                :, piece * LANES : (piece + 1) * LANES
            ]
    for out, other in ((send, core ^ 1), (keep, core)):
        for b in range(2):
            for c in range(2):
                out[b, c, :IN_SENT] = blocks[(y ^ (3 * b) ^ c) * 2 + other]
    send[:, :, IN_SENT:] = jnp.zeros((2, 2, SENT_ROWS - IN_SENT, LANES), jnp.float32)


def output_kernel(table, grads, send, keep):
    x = lax.axis_index("x")
    for b, out in ((1, send), (0, keep)):
        for c in range(2):
            out[c] = jnp.dot(
                table[...], grads[x ^ b ^ (3 * c)], preferred_element_type=jnp.float32
            )


def add_kernel(own, got, after, send, keep):
    keep[...] = own[0] + got[0]
    send[...] = own[1] + got[1]


def add_core_kernel(own, got, send, keep):
    keep[...] = own[0] + got[0, :, :IN_SENT]
    send[:, :IN_SENT] = own[1] + got[1, :, :IN_SENT]
    send[:, IN_SENT:] = jnp.zeros((2, PADDED_ROWS - IN_SENT, LANES), jnp.float32)


def add_y_kernel(own, got, after, send, keep):
    keep[...] = own[0] + got[0, :IN_SENT]
    send[...] = own[1] + got[1, :IN_SENT]


def pack_kernel(in_own, in_got, out_own, out_got, packed):
    side_in = in_own[...] + in_got[...]
    side_out = out_own[...] + out_got[...]
    for dest in range(8):
        half = (dest % 2) * OUT_HERE
        packed[dest, :OUT_HERE] = side_out[half : half + OUT_HERE]
        half = (dest // 4) * IN_HERE
        packed[dest, OUT_HERE:] = side_in[half : half + IN_HERE]


def feature_kernel(packed, spread):
    factor_half = lax.axis_index("za")
    sides_in, sides_out = [], []
    for z in range(2):
        sides_out.append(
            (packed[z, :OUT_HERE] + packed[2 + z, :OUT_HERE])
            + (packed[4 + z, :OUT_HERE] + packed[6 + z, :OUT_HERE])
        )
        source = factor_half * 4 + z * 2
        sides_in.append(packed[source, OUT_HERE:] + packed[source + 1, OUT_HERE:])
    product = lax.dot_general(
        jnp.concatenate(sides_in, axis=1) * SEQ_LEN ** (-0.5),
        jnp.concatenate(sides_out, axis=1),
        (((1,), (1,)), ((), ())),
        precision=lax.Precision.HIGHEST,
        preferred_element_type=jnp.float32,
    )
    total = jnp.concatenate(
        [product, jnp.zeros((IN_HERE, LANES - OUT_HERE), jnp.float32)], axis=1
    )
    for place in range(8):
        moved = total if place == 0 else pltpu.roll(total, LANES - 4 * place, 1)
        spread[place % 2 * 4 + place // 2] = moved


def sum_kernel(parts, features):
    total = parts[0]
    for place in range(1, 8):
        total = total + parts[place]
    for seq in range(SEQS):
        features[seq] = total[2 * seq : 2 * seq + 2, :4]


def body(activations, out_grads, hash_seeds, offsets):
    acts = jnp.swapaxes(activations, 1, 2)
    grads = jnp.swapaxes(out_grads, 1, 2)
    here_in = acts.shape[1]
    vmem = pl.BlockSpec(memory_space=pltpu.VMEM)
    hbm = pl.BlockSpec(memory_space=pltpu.HBM)
    anywhere = pl.BlockSpec(memory_space=pl.ANY)
    params = pltpu.CompilerParams(vmem_limit_bytes=16 * 1024 * 1024)

    def shaped(*dims):
        return jax.ShapeDtypeStruct(dims, jnp.float32)

    def pinned(value):
        return pltpu.with_memory_space_constraint(value, pltpu.HBM)

    def swap(value, axis, distance):
        size = SIZES[AXES.index(axis)]
        return lax.ppermute(value, axis, [(i, i ^ distance) for i in range(size)])

    def add(own, got, after, name):
        return pl.pallas_call(
            add_kernel,
            out_shape=[shaped(*own.shape[1:])] * 2,
            in_specs=[vmem, vmem, anywhere],
            out_specs=[vmem] * 2,
            compiler_params=params,
            name=name,
        )(own, got, after)

    in_send, in_keep, out_table = pl.pallas_call(
        input_kernel,
        out_shape=[shaped(2, 2, SENT_ROWS, LANES), shaped(2, 2, IN_SENT, LANES)]
        + [jax.ShapeDtypeStruct((K_OUT, grads.shape[1]), jnp.bfloat16)],
        in_specs=[hbm] * 3,
        out_specs=[vmem] * 3,
        scratch_shapes=[
            pltpu.SMEM((2,), jnp.int32),
            pltpu.SMEM((2,), jnp.int32),
            pltpu.VMEM((PARTS, here_in, PART), jnp.bfloat16),
            pltpu.VMEM((BLOCKS // 2, IN_SENT, LANES), jnp.float32),
            pltpu.SemaphoreType.DMA((PARTS,)),
            pltpu.SemaphoreType.DMA((2,)),
        ],
        compiler_params=params,
        name="input_terms",
    )(pinned(hash_seeds), pinned(offsets), pinned(acts))
    in_got = swap(in_send, "core", 1)
    out_send, out_keep = pl.pallas_call(
        output_kernel,
        out_shape=[shaped(2, K_OUT, LANES)] * 2,
        in_specs=[vmem] * 2,
        out_specs=[vmem] * 2,
        compiler_params=params,
        name="output_terms",
    )(out_table, grads)
    in_send, in_keep = pl.pallas_call(
        add_core_kernel,
        out_shape=[shaped(2, PADDED_ROWS, LANES), shaped(2, IN_SENT, LANES)],
        in_specs=[vmem] * 2,
        out_specs=[vmem] * 2,
        compiler_params=params,
        name="add_core",
    )(in_keep, in_got)
    in_got = swap(in_send, "y", 3)
    out_got = swap(out_send, "x", 1)
    out_send, out_keep = add(out_keep, out_got, in_send, "add_x")
    out_got = swap(out_send, "x", 3)
    in_send, in_keep = pl.pallas_call(
        add_y_kernel,
        out_shape=[shaped(IN_SENT, LANES)] * 2,
        in_specs=[vmem, vmem, anywhere],
        out_specs=[vmem] * 2,
        compiler_params=params,
        name="add_y",
    )(in_keep, in_got, out_send)
    in_got = swap(in_send, "y", 1)
    packed = pl.pallas_call(
        pack_kernel,
        out_shape=shaped(8, OUT_HERE + IN_HERE, LANES),
        in_specs=[vmem] * 4,
        out_specs=vmem,
        compiler_params=params,
        name="pack_sides",
    )(in_keep, in_got, out_keep, out_got)
    packed = lax.all_to_all(packed, ("zb", "za", "zh"), 0, 0, tiled=True)
    spread = pl.pallas_call(
        feature_kernel,
        out_shape=shaped(8, 8, LANES),
        in_specs=[vmem],
        out_specs=vmem,
        compiler_params=params,
        name="feature_partials",
    )(packed)
    spread = lax.all_to_all(
        spread.reshape(32, 2, LANES), ("core", "y", "x"), 0, 0, tiled=True
    )
    summed = jnp.sum(spread.reshape(8, SEQS, 2, LANES), axis=0)
    return summed[:, :, :4]


def solution(mesh):
    fine = Mesh(mesh.devices.reshape(SIZES), AXES)
    return jax.shard_map(
        body,
        mesh=fine,
        in_specs=(P(None, None, ROW), P(None, ROW, COL), P(), P()),
        out_specs=P(None, COL, ROW),
        check_vma=False,
    )
```
